256 devices in a mesh: tm: 16 (over z, core), space: 16 (over y, x).
Axes of the slice: x: 4, y: 4, z: 8, core: 2. Of those that a mesh axis runs over, the one named last changes fastest.
Arguments:
- forcing: float32 [128, 64, 32, 128], P('tm', 'space'), may hold values from -6 to 6
- c_guess: float32 [32, 64, 32, 128], P('tm', 'space'), may hold values from -6 to 6
- initial: float32 [64, 32, 128], P('space'), may hold values from -6 to 6
- porosity: float32 [64, 32, 128], P('space'), may hold values from 0.5 to 4
- permeability: float32 [3, 64, 32, 128], P(None, 'space'), may hold values from 0.1 to 10
Outputs:
- fine_state: float32 [128, 64, 32, 128], P('tm', 'space')
- coarse_state: float32 [32, 64, 32, 128], P('tm', 'space')
- coarse_source: float32 [16, 64, 32, 128], P('tm', 'space')
The draws below stay inside these ranges and needn't reach their ends.
All inputs are finite; a program needn't handle non-finite values.
Results may differ from the reference program's by a relative error of at most 0.00002.
Values sent between devices are 32-bit elements; how exact they have to be, the bound alone decides.
No kernel may reach another device: no remote copies, remote signals or barrier semaphores. Data moves between devices by JAX's collectives and lax.ppermute only.
A program may use at most 64 MiB of HBM per device.

```python
import math
import jax
import jax.numpy as jnp
from jax import lax

NX = 128
NY = 32
CF = 4
SWEEPS = 4
NZ = 64
NT = 128


def level_of(own_key, extent, shards, low, largest):
    def one(axis_at, blocks):
        heights = jax.random.uniform(jax.random.fold_in(jax.random.fold_in(own_key, 6), axis_at), (blocks,), jnp.float32, low / len(shards), largest / len(shards))
        return jnp.repeat(jnp.exp(heights), extent[axis_at] // blocks).reshape((-1,) + (1,) * (len(extent) - axis_at - 1))

    loudness = one(*shards[0])
    for cut in shards[1:]:
        loudness = loudness * one(*cut)
    return loudness


def normal_values(rng, shape, scale, bound, cuts=(), held_as=jnp.bfloat16):
    gain = level_of(rng, shape, cuts, -0.22, 0.18) if cuts else 1.0
    drawn = jax.random.normal(rng, shape, jnp.float32) * scale * gain
    return jnp.minimum(jnp.maximum(drawn, -bound), bound).astype(held_as)


def setup_inputs(seed: int = 0) -> dict:
    arg_keys = jax.random.split(jax.random.key(seed), 6)
    forcing = normal_values(arg_keys[0], (NT, NZ, NY, NX), 1.0, 6.0, ((0, 16), (1, 16)), jnp.float32)
    c_guess = normal_values(arg_keys[1], (NT // CF, NZ, NY, NX), 1.0, 6.0, ((0, 16), (1, 16)), jnp.float32)
    initial = normal_values(arg_keys[2], (NZ, NY, NX), 1.0, 6.0, ((0, 16),), jnp.float32)
    porosity = jnp.clip(jnp.exp(math.log(4.0) - 2.0794415 * jax.random.uniform(arg_keys[3], (NZ, NY, NX), jnp.float32) ** level_of(arg_keys[3], (NZ, NY, NX), ((0, 16),), -0.2, 0.2)), 0.5, 4.0)
    permeability = jnp.clip(jnp.exp(math.log(10.0) - 4.6051702 * jax.random.uniform(arg_keys[4], (3, NZ, NY, NX), jnp.float32) ** level_of(arg_keys[4], (3, NZ, NY, NX), ((1, 16),), -0.2, 0.2)), 0.1, 10.0)
    return dict(forcing=forcing, c_guess=c_guess, initial=initial, porosity=porosity, permeability=permeability)


storage_rate = 2.0


def harmonic_faces(padded, dimension):
    length = padded.shape[dimension]
    lower_k = lax.slice_in_dim(padded, 0, length - 1, axis=dimension)
    upper_k = lax.slice_in_dim(padded, 1, length, axis=dimension)
    faces = 2.0 * lower_k * upper_k / (lower_k + upper_k)
    count = length - 1
    return lax.slice_in_dim(faces, 0, count - 1, axis=dimension), lax.slice_in_dim(faces, 1, count, axis=dimension)


def faces_along(perm_k, dimension):
    length = perm_k.shape[dimension]
    leading = lax.slice_in_dim(perm_k, 0, 1, axis=dimension)
    trailing = lax.slice_in_dim(perm_k, length - 1, length, axis=dimension)
    return harmonic_faces(jnp.concatenate([leading, perm_k, trailing], dimension), dimension)


def lower_upper(field, dimension):
    dimension = dimension % field.ndim
    length = field.shape[dimension]
    empty = jnp.zeros_like(lax.slice_in_dim(field, 0, 1, axis=dimension))
    lower = jnp.concatenate([empty, lax.slice_in_dim(field, 0, length - 1, axis=dimension)], dimension)
    upper = jnp.concatenate([lax.slice_in_dim(field, 1, length, axis=dimension), empty], dimension)
    return lower, upper


def relax_sweep(center, z_lower, z_upper, right_side, coefficients, inverse_diag):
    west, east, south, north, below, above = coefficients
    x_lower, x_upper = lower_upper(center, -1)
    y_lower, y_upper = lower_upper(center, -2)
    total = right_side + (west * x_lower + east * x_upper) + (south * y_lower + north * y_upper) + (below * z_lower + above * z_upper)
    return total * inverse_diag


def reference(forcing, c_guess, initial, porosity, permeability):
    west, east = faces_along(permeability[0], 2)
    south, north = faces_along(permeability[1], 1)
    below, above = faces_along(permeability[2], 0)
    coefficients = (west, east, south, north, below, above)
    coupling = ((west + east) + (south + north)) + (below + above)
    storage = porosity * storage_rate

    def advance(state, source_term, factor):
        storage_now = storage * factor
        inverse_diag = 1.0 / (storage_now + coupling)
        right_side = storage_now * state + source_term
        iterate = state
        for sweep in range(SWEEPS):
            z_lower, z_upper = lower_upper(iterate, 0)
            iterate = relax_sweep(iterate, z_lower, z_upper, right_side, coefficients, inverse_diag)
        return iterate

    block_count = NT // CF
    blocks = forcing.reshape(block_count, CF, NZ, NY, NX)
    empty = jnp.zeros_like(initial)

    def frelax(args):
        current = args[0]
        results = []
        for section in range(CF - 1):
            current = advance(current, args[1][section], 1.0)
            results.append(current)
        return jnp.stack(results)

    previous = jnp.concatenate([initial[None], c_guess[:-1]], 0)
    early_fine = lax.map(frelax, (previous, blocks))
    relaxed_c = lax.map(lambda args: advance(args[0], args[1][CF - 1], 1.0), (early_fine[:, CF - 2], blocks))
    previous_c = jnp.concatenate([initial[None], relaxed_c[:-1]], 0)
    late_fine = lax.map(frelax, (previous_c, blocks))
    fine_state = jnp.concatenate([late_fine, relaxed_c[:, None]], 1).reshape(NT, NZ, NY, NX)
    residual = lax.map(lambda args: advance(args[0], args[1][CF - 1], 1.0) - args[2], (late_fine[:, CF - 2], blocks, relaxed_c))
    coarse_prev = lax.map(lambda state: advance(state, empty, 1.0 / CF), previous_c)
    level_source = (residual + relaxed_c) - coarse_prev

    def coarse_step(state):
        return advance(state, empty, 1.0 / CF)

    pair_count = block_count // 2
    source_pairs = level_source.reshape(pair_count, 2, NZ, NY, NX)
    start = previous_c.reshape(pair_count, 2, NZ, NY, NX)[:, 0]
    coarse_first = lax.map(coarse_step, start) + source_pairs[:, 0]
    coarse_last = lax.map(coarse_step, coarse_first) + source_pairs[:, 1]
    previous_two = jnp.concatenate([initial[None], coarse_last[:-1]], 0)
    coarse_again = lax.map(coarse_step, previous_two) + source_pairs[:, 0]
    coarse_state = jnp.stack([coarse_again, coarse_last], 1).reshape(block_count, NZ, NY, NX)
    second_residual = (lax.map(coarse_step, coarse_again) + source_pairs[:, 1]) - coarse_last
    coarsest_prev = lax.map(lambda state: advance(state, empty, 1.0 / (2 * CF)), previous_two)
    coarse_source = (second_residual + coarse_last) - coarsest_prev
    return fine_state, coarse_state, coarse_source
```

```python
import jax
import jax.numpy as jnp
from jax import lax
from jax.sharding import PartitionSpec as P

CF = 4
SWEEPS = 4
SLAB = 4
REACH = 8

storage_rate = 2.0


def shifted(value, dt, ds):
    times = lax.axis_size("tm")
    slabs = lax.axis_size("space")
    pairs = [
        (t * slabs + s, ((t + dt) % times) * slabs + (s + ds) % slabs)
        for t in range(times)
        for s in range(slabs)
    ]
    return lax.ppermute(value, ("tm", "space"), pairs)


def faces(padded, dimension):
    length = padded.shape[dimension]
    lower_k = lax.slice_in_dim(padded, 0, length - 1, axis=dimension)
    upper_k = lax.slice_in_dim(padded, 1, length, axis=dimension)
    both = 2.0 * lower_k * upper_k / (lower_k + upper_k)
    count = length - 1
    return (
        lax.slice_in_dim(both, 0, count - 1, axis=dimension),
        lax.slice_in_dim(both, 1, count, axis=dimension),
    )


def faces_along(perm_k, dimension):
    length = perm_k.shape[dimension]
    leading = lax.slice_in_dim(perm_k, 0, 1, axis=dimension)
    trailing = lax.slice_in_dim(perm_k, length - 1, length, axis=dimension)
    return faces(jnp.concatenate([leading, perm_k, trailing], dimension), dimension)


def sweep(center, right_side, coefficients, margin):
    west, east, south, north, below, above, inverse_diag = [
        lax.slice_in_dim(c, REACH - 1 - margin, REACH - 1 + SLAB + margin, axis=0)
        for c in coefficients
    ]
    middle = center[..., 1:-1, :, :]
    x_lower, x_upper = jnp.roll(middle, 1, -1), jnp.roll(middle, -1, -1)
    y_lower, y_upper = jnp.roll(middle, 1, -2), jnp.roll(middle, -1, -2)
    total = (
        right_side
        + (west * x_lower + east * x_upper)
        + (south * y_lower + north * y_upper)
        + (below * center[..., :-2, :, :] + above * center[..., 2:, :, :])
    )
    return total * inverse_diag


def advance(window, source, storage, coefficients, margin):
    storage_now = lax.slice_in_dim(
        storage, REACH - 4 - margin, REACH + 2 + SLAB + margin, axis=0
    )
    right_side = storage_now * window[..., 1:-1, :, :]
    if source is not None:
        right_side = right_side + source
    iterate = window
    for step in range(SWEEPS):
        inner = right_side.shape[-3]
        now = right_side[..., step : inner - step, :, :]
        iterate = sweep(iterate, now, coefficients, margin + 3 - step)
    return iterate


def on_device(forcing, c_guess, initial, porosity, permeability):
    cells = initial.shape[1:]
    blocks = forcing.reshape((2, CF) + initial.shape)
    times = lax.axis_size("tm")
    slabs = lax.axis_size("space")
    last_time = lax.axis_index("tm") == times - 1
    position = lax.axis_index("space")

    fields = jnp.concatenate([permeability, porosity[None]], 0)

    guess_on = jnp.where(last_time, initial, c_guess[1])
    up = jnp.concatenate([c_guess[0], blocks[:, :, 1:].reshape((-1,) + cells), fields.reshape((-1,) + cells)], 0)
    down = jnp.concatenate([c_guess[0], blocks[:, :, :3].reshape((-1,) + cells), fields.reshape((-1,) + cells)], 0)
    from_below = shifted(up, 0, 1)
    from_above = shifted(down, 0, -1)
    previous_0 = jnp.concatenate([shifted(guess_on, 1, 1), shifted(guess_on, 1, 0), shifted(guess_on, 1, -1)], 0)
    previous_1 = jnp.concatenate([from_below[:4], c_guess[0], from_above[:4]], 0)
    previous = jnp.stack([previous_0, previous_1])
    wide_blocks = jnp.concatenate(
        [from_below[4:28].reshape((2, CF, 3) + cells), blocks, from_above[4:28].reshape((2, CF, 3) + cells)], 2
    )
    far_below = shifted(fields, 0, 2)
    far_above = shifted(fields, 0, -2)
    wide = jnp.concatenate(
        [far_below, from_below[28:].reshape((4, SLAB) + cells), fields, from_above[28:].reshape((4, SLAB) + cells), far_above], 1
    )

    west, east = faces_along(wide[0][1:-1], 2)
    south, north = faces_along(wide[1][1:-1], 1)
    perm_z = wide[2]
    both = 2.0 * perm_z[:-1] * perm_z[1:] / (perm_z[:-1] + perm_z[1:])
    plane = lax.broadcasted_iota(jnp.int32, (SLAB + 2 * REACH - 2, 1, 1), 0)
    height = position * SLAB + plane - (REACH - 1)
    at_floor = height == 0
    at_top = height == slabs * SLAB - 1
    inner_z = perm_z[1:-1]
    below = jnp.where(at_floor, inner_z, both[:-1])
    above = jnp.where(at_top, inner_z, both[1:])
    coupling = ((west + east) + (south + north)) + (below + above)
    storage = wide[3][1:-1] * storage_rate
    column = lax.broadcasted_iota(jnp.int32, (1, 1, cells[1]), 2)
    row = lax.broadcasted_iota(jnp.int32, (1, cells[0], 1), 1)
    links = (
        jnp.where(column == 0, 0.0, west),
        jnp.where(column == cells[1] - 1, 0.0, east),
        jnp.where(row == 0, 0.0, south),
        jnp.where(row == cells[0] - 1, 0.0, north),
        jnp.where(at_floor, 0.0, below),
        jnp.where(at_top, 0.0, above),
    )

    def scaled(factor):
        storage_now = storage * factor
        return storage_now, links + (1.0 / (storage_now + coupling),)

    fine = scaled(1.0)
    coarse = scaled(1.0 / CF)
    coarsest = scaled(1.0 / (2 * CF))

    def widened(value):
        return jnp.concatenate([shifted(value[:, -4:], 0, 1), value, shifted(value[:, :4], 0, -1)], 1)

    window = previous
    early = []
    for section in range(CF):
        current = advance(window, wide_blocks[:, section], *fine, 0)
        early.append(current)
        if section < CF - 1:
            window = widened(current)
    relaxed_c = early[-1]

    relaxed_on = jnp.where(last_time, initial, relaxed_c[1])
    previous_c0 = jnp.concatenate(
        [shifted(relaxed_on, 1, 1), shifted(relaxed_on, 1, 0), shifted(relaxed_on, 1, -1)], 0
    )
    previous_c1 = jnp.concatenate(
        [shifted(relaxed_c[0], 0, 1), relaxed_c[0], shifted(relaxed_c[0], 0, -1)], 0
    )
    window = jnp.stack([previous_c0, previous_c1]) - previous
    late = []
    for section in range(CF):
        change = advance(window, None, *fine, 0)
        if section < CF - 1:
            late.append(early[section] + change)
            window = widened(change)
    fine_state = jnp.stack(late + [relaxed_c], 1).reshape(forcing.shape)
    again_c = relaxed_c + change

    near = widened(change)
    low = shifted(change[0], 0, 2)
    high = shifted(change[0], 0, -2)
    corrected = advance(jnp.concatenate([low, near[0], high], 0), None, *coarse, 4)
    coarse_last = again_c[1] + corrected[4:8]
    shift_on = jnp.where(last_time, 0.0, near[1] + corrected)
    shift_low = shifted(shift_on, 1, 1)
    shift_high = shifted(shift_on, 1, -1)
    own = jnp.where(position == 0, shift_high[:4], shift_low[8:])
    epsilon = jnp.concatenate([shift_low[:8], own, shift_high[4:]], 0)
    previous_two = previous_c0 + epsilon[4:-4]
    first = advance(epsilon, None, *coarse, 4)
    coarse_again = again_c[0] + first[4:8]
    second = advance(first, None, *coarse, 0)
    third = advance(previous_two, None, *coarsest, 0)
    coarse_state = jnp.stack([coarse_again, coarse_last])
    coarse_source = (second + coarse_last) - third
    return (fine_state, coarse_state, coarse_source[None])


def solution(mesh):
    return jax.shard_map(
        on_device,
        mesh=mesh,
        in_specs=(
            P("tm", "space", None, None),
            P("tm", "space", None, None),
            P("space", None, None),
            P("space", None, None),
            P(None, "space", None, None),
        ),
        out_specs=(
            P("tm", "space", None, None),
            P("tm", "space", None, None),
            P("tm", "space", None, None),
        ),
        check_vma=False,
    )
```

```python
import jax
import jax.numpy as jnp
from jax import lax
from jax.experimental import pallas as pl
from jax.experimental.pallas import tpu as pltpu
from jax.sharding import PartitionSpec as P

CF = 4
SLAB = 4
EDGE = SLAB - 1
ROWS = 4

storage_rate = 2.0


def shifted(value, dt, ds):
    times = lax.axis_size("tm")
    slabs = lax.axis_size("space")
    pairs = [
        (t * slabs + s, ((t + dt) % times) * slabs + (s + ds) % slabs)
        for t in range(times)
        for s in range(slabs)
    ]
    return lax.ppermute(value, ("tm", "space"), pairs)


def call(kernel, name, outs, *args, scratch=()):
    in_vmem = [pltpu.with_memory_space_constraint(a, pltpu.VMEM) for a in args]
    spec = pl.BlockSpec(memory_space=pltpu.VMEM)
    return pl.pallas_call(
        kernel,
        out_shape=[pltpu.VMEM(shape, jnp.float32) for shape in outs],
        in_specs=[spec] * len(args),
        out_specs=[spec] * len(outs),
        scratch_shapes=[pltpu.VMEM(shape, jnp.float32) for shape in scratch],
        name=name,
        compiler_params=pltpu.CompilerParams(vmem_limit_bytes=16 * 2**20),
    )(*in_vmem)


PLANE = (ROWS, 8, 128)


def plane_of(ref, *at):
    return [ref[(*at, pl.ds(j, 8, stride=ROWS), slice(None))] for j in range(ROWS)]


def put_plane(ref, at, rows):
    for j in range(ROWS):
        ref[(*at, pl.ds(j, 8, stride=ROWS), slice(None))] = rows[j]


def x_lower(v):
    return pltpu.roll(v, 1, 1)


def x_upper(v):
    return pltpu.roll(v, 127, 1)


def y_lower(rows):
    return [pltpu.roll(rows[-1], 1, 0)] + rows[:-1]


def y_upper(rows):
    return rows[1:] + [pltpu.roll(rows[0], 7, 0)]


def rows_at(ref, *at):
    return [ref[(*at, j)] for j in range(ROWS)]


def put_rows(ref, at, rows):
    for j in range(ROWS):
        ref[(*at, j)] = rows[j]


WEST, EAST, SOUTH, NORTH, BELOW, ABOVE, STORAGE, FINE, COARSE, COARSEST = range(10)
REACH = SLAB + 2 * EDGE
FACTORS = {FINE: 1.0, COARSE: 1.0 / CF, COARSEST: 1.0 / (2 * CF)}


def step(coef, levels, window, source, put, near, far, right):
    count = len(levels)
    for turn in range(4):
        planes = REACH - 2 * turn
        out = [near, far, near, None][turn]
        held = [None, near, far, near][turn]
        for p in range(planes):
            at = p + turn
            links = [rows_at(coef, kind, at) for kind in range(6)]
            inverses = {level: rows_at(coef, level, at) for level in set(levels)}
            for b in range(count):
                if turn == 0:
                    lower, middle, upper = window(b, p), window(b, p + 1), window(b, p + 2)
                    stored = rows_at(coef, STORAGE, at)
                    factor = FACTORS[levels[b]]
                    if factor != 1.0:
                        stored = [s * factor for s in stored]
                    rhs = [s * v for s, v in zip(stored, middle)]
                    if source is not None:
                        rhs = [r + f for r, f in zip(rhs, source(b, p))]
                    if 0 < p < planes - 1:
                        put_rows(right, (b, p - 1), rhs)
                else:
                    lower, middle, upper = [rows_at(held, b, p + k) for k in range(3)]
                    rhs = rows_at(right, b, at - 1)
                south_of, north_of = y_lower(middle), y_upper(middle)
                result = []
                for j in range(ROWS):
                    west, east, south, north, below, above = [link[j] for link in links]
                    total = rhs[j] + (west * x_lower(middle[j]) + east * x_upper(middle[j]))
                    total = total + (south * south_of[j] + north * north_of[j])
                    total = total + (below * lower[j] + above * upper[j])
                    result.append(total * inverses[levels[b]][j])
                if out is None:
                    put(b, p, result)
                else:
                    put_rows(out, (b, p), result)


def scratch_of(count):
    return [(count, 10) + PLANE, (count, 8) + PLANE, (count, 8) + PLANE]


def windows(lo, own, hi):
    def window(b, p):
        if p < SLAB:
            return rows_at(lo, b, p)
        if p < 2 * SLAB:
            return rows_at(own, b, p - SLAB)
        return rows_at(hi, b, p - 2 * SLAB)

    return window


UP_GUESS, UP_FORCE, UP_X, UP_Y, UP_PORE, UP_Z = 0, 4, 10, 13, 16, 19
MESSAGE = 23


def prepare_kernel(forcing, guess, initial, porosity, permeability, up, down, up_later, down_later, on, own_force, own_guess, own_field):
    last_time = lax.axis_index("tm") == lax.axis_size("tm") - 1
    for z in range(SLAB):
        for b in range(2):
            for i in range(CF):
                rows = plane_of(forcing, b * CF + i, z)
                put_rows(own_force, (b, i, z), rows)
                for target, later, skip in ((up, up_later, 1), (down, down_later, 0)):
                    if 0 <= z - skip < EDGE:
                        if i == 0:
                            put_rows(target, (UP_FORCE + EDGE * b + z - skip,), rows)
                        else:
                            put_rows(later, (b, i - 1, z - skip), rows)
        rows = plane_of(guess, 0, z)
        put_rows(own_guess, (z,), rows)
        put_rows(up, (UP_GUESS + z,), rows)
        put_rows(down, (UP_GUESS + z,), rows)
        first, other = plane_of(initial, z), plane_of(guess, 1, z)
        put_rows(on, (z,), [jnp.where(last_time, a, b) for a, b in zip(first, other)])
        for kind in range(4):
            rows = plane_of(permeability, kind, z) if kind < 3 else plane_of(porosity, z)
            put_rows(own_field, (kind, z), rows)
            start = [UP_X, UP_Y, UP_Z, UP_PORE][kind]
            for target, skip in ((up, 1), (down, 0)):
                if kind == 2:
                    put_rows(target, (start + z,), rows)
                elif 0 <= z - skip < EDGE:
                    put_rows(target, (start + z - skip,), rows)


def harmonic(lower, upper):
    return [2.0 * a * b / (a + b) for a, b in zip(lower, upper)]


def coefficients(lo, hi, field, coef):
    position = lax.axis_index("space")
    column = lax.broadcasted_iota(jnp.int32, (8, 128), 1)
    row = lax.broadcasted_iota(jnp.int32, (8, 128), 0)
    zero = jnp.zeros((8, 128), jnp.float32)

    def held(kind, p):
        start = [UP_X, UP_Y, UP_Z, UP_PORE][kind]
        if kind == 2:
            p, width = p + 1, SLAB
        else:
            width = EDGE
        if p < width:
            return rows_at(lo, start + p)
        if p < width + SLAB:
            return rows_at(field, kind, p - width)
        return rows_at(hi, start + p - width - SLAB)

    above_before = None
    for p in range(REACH):
        kx, ky, kz, pore = [held(kind, p) for kind in range(4)]
        side = harmonic(kx, [x_upper(k) for k in kx])
        east_link = [jnp.where(column == 127, zero, v) for v in side]
        east = [jnp.where(column == 127, k, v) for k, v in zip(kx, side)]
        side = [x_lower(v) for v in side]
        west_link = [jnp.where(column == 0, zero, v) for v in side]
        west = [jnp.where(column == 0, k, v) for k, v in zip(kx, side)]
        side = harmonic(ky, y_upper(ky))
        north_link, north = list(side), list(side)
        north_link[-1] = jnp.where(row == 7, zero, side[-1])
        north[-1] = jnp.where(row == 7, ky[-1], side[-1])
        side = y_lower(side)
        south_link, south = list(side), list(side)
        south_link[0] = jnp.where(row == 0, zero, side[0])
        south[0] = jnp.where(row == 0, ky[0], side[0])
        below_link = below = above_before if p else harmonic(held(2, p - 1), kz)
        above_link = above = above_before = harmonic(kz, held(2, p + 1))
        if p == EDGE:
            floor = position == 0
            below = [jnp.where(floor, k, v) for k, v in zip(kz, below)]
            below_link = [jnp.where(floor, zero, v) for v in below_link]
        if p == EDGE + SLAB - 1:
            top = position == lax.axis_size("space") - 1
            above = [jnp.where(top, k, v) for k, v in zip(kz, above)]
            above_link = [jnp.where(top, zero, v) for v in above_link]
        for kind, rows in enumerate([west_link, east_link, south_link, north_link, below_link, above_link]):
            put_rows(coef, (kind, p), rows)
        stored = [storage_rate * v for v in pore]
        put_rows(coef, (STORAGE, p), stored)
        for j in range(ROWS):
            coupling = ((west[j] + east[j]) + (south[j] + north[j])) + (below[j] + above[j])
            for level, factor in FACTORS.items():
                coef[level, p, j] = 1.0 / (stored[j] * factor + coupling)


def first_kernel(guess, low, mid, high, lo, hi, force, field, coef, state, near, far, right):
    coefficients(lo, hi, field, coef)

    def window(b, p):
        part, at = divmod(p, SLAB)
        if b == 0:
            return rows_at([low, mid, high][part], at)
        return rows_at([lo, guess, hi][part], at)

    def source(b, p):
        if p < EDGE:
            return rows_at(lo, UP_FORCE + EDGE * b + p)
        if p < EDGE + SLAB:
            return rows_at(force, b, 0, p - EDGE)
        return rows_at(hi, UP_FORCE + EDGE * b + p - EDGE - SLAB)

    step(coef, [FINE, FINE], window, source, lambda b, p, rows: put_rows(state, (b, p), rows), near, far, right)


def early_kernel(section):
    def kernel(own, lo, hi, force, force_lo, force_hi, coef, state, near, far, right):
        def source(b, p):
            if p < EDGE:
                return rows_at(force_lo, b, section - 1, p)
            if p < EDGE + SLAB:
                return rows_at(force, b, section, p - EDGE)
            return rows_at(force_hi, b, section - 1, p - EDGE - SLAB)

        put = lambda b, p, rows: put_rows(state, (b, p), rows)
        step(coef, [FINE, FINE], windows(lo, own, hi), source, put, near, far, right)

    return kernel


def pass_kernel(relaxed, initial, on):
    last_time = lax.axis_index("tm") == lax.axis_size("tm") - 1
    for z in range(SLAB):
        rows = [jnp.where(last_time, a, b) for a, b in zip(plane_of(initial, z), rows_at(relaxed, 1, z))]
        put_rows(on, (z,), rows)


def change_kernel(arrived, mid, relaxed, guess, change):
    for z in range(SLAB):
        for j in range(ROWS):
            change[0, z, j] = arrived[z, j] - mid[z, j]
            change[1, z, j] = relaxed[0, z, j] - guess[z, j]


def late_kernel(own, lo, hi, coef, state, near, far, right):
    put = lambda b, p, rows: put_rows(state, (b, p), rows)
    step(coef, [FINE, FINE], windows(lo, own, hi), None, put, near, far, right)


def fine_kernel(early0, early1, early2, relaxed, late0, late1, late2, fine):
    for b in range(2):
        for z in range(SLAB):
            for i, (early, late) in enumerate(((early0, late0), (early1, late1), (early2, late2))):
                rows = [u + d for u, d in zip(rows_at(early, b, z), rows_at(late, b, z))]
                put_plane(fine, (b * CF + i, z), rows)
            put_plane(fine, (b * CF + CF - 1, z), rows_at(relaxed, b, z))


def last_kernel(change, lo, hi, relaxed, coef, last, on, near, far, right):
    last_time = lax.axis_index("tm") == lax.axis_size("tm") - 1

    def window(b, p):
        part, at = divmod(p, SLAB)
        return rows_at(change, 0, at) if part == 1 else rows_at([lo, None, hi][part], at)

    def put(b, p, rows):
        moved = rows_at(change, 1, p)
        rows = [a + d for a, d in zip(moved, rows)]
        put_rows(last, (p,), [u + d for u, d in zip(rows_at(relaxed, 1, p), rows)])
        put_rows(on, (p,), [jnp.where(last_time, 0.0, d) for d in rows])

    step(coef, [COARSE], window, None, put, near, far, right)


def again_kernel(
    low, mid, high, start_lo, start_hi, change_lo, change_hi, arrived, change, relaxed, coef,
    moved, again, third, near, far, right,
):
    def window(b, p):
        part, at = divmod(p, SLAB)
        epsilon = rows_at([low, mid, high][part], at)
        if b == 0:
            return epsilon
        if part == 1:
            start = rows_at(arrived, at)
        else:
            start = [
                u + d
                for u, d in zip(
                    rows_at([start_lo, None, start_hi][part], at), rows_at([change_lo, None, change_hi][part], 0, at)
                )
            ]
        return [u + e for u, e in zip(start, epsilon)]

    def put(b, p, rows):
        if b == 0:
            put_rows(moved, (p,), rows)
            point = [u + d for u, d in zip(rows_at(relaxed, 0, p), rows_at(change, 0, p))]
            put_rows(again, (p,), [u + d for u, d in zip(point, rows)])
        else:
            put_rows(third, (p,), rows)

    step(coef, [COARSE, COARSEST], window, None, put, near, far, right)


def source_kernel(moved, lo, hi, last, again, third, coef, state, source, near, far, right):
    def window(b, p):
        part, at = divmod(p, SLAB)
        return rows_at([lo, moved, hi][part], at)

    def put(b, p, rows):
        point = rows_at(last, p)
        put_plane(source, (0, p), [(d + u) - w for d, u, w in zip(rows, point, rows_at(third, p))])
        put_plane(state, (1, p), point)
        put_plane(state, (0, p), rows_at(again, p))

    step(coef, [COARSE], window, None, put, near, far, right)


def on_device(forcing, c_guess, initial, porosity, permeability):
    four = (SLAB,) + PLANE
    both = (2,) + four

    up, down, up_later, down_later, on, force, guess, field = call(
        prepare_kernel,
        "prepare",
        [
            (MESSAGE,) + PLANE,
            (MESSAGE,) + PLANE,
            (2, CF - 1, EDGE) + PLANE,
            (2, CF - 1, EDGE) + PLANE,
            four,
            (2, CF) + four,
            four,
            (4,) + four,
        ],
        forcing,
        c_guess,
        initial,
        porosity,
        permeability,
    )
    lo, hi = shifted(up, 0, 1), shifted(down, 0, -1)
    low, mid, high = shifted(on, 1, 1), shifted(on, 1, 0), shifted(on, 1, -1)
    force_lo, force_hi = shifted(up_later, 0, 1), shifted(down_later, 0, -1)
    coef, state = call(
        first_kernel, "first", [(10, REACH) + PLANE, both], guess, low, mid, high, lo, hi, force, field,
        scratch=scratch_of(2),
    )
    early = [state]
    for section in range(1, CF):
        state_lo, state_hi = shifted(state, 0, 1), shifted(state, 0, -1)
        (state,) = call(
            early_kernel(section), f"early{section}", [both], state, state_lo, state_hi, force, force_lo, force_hi,
            coef, scratch=scratch_of(2),
        )
        early.append(state)
    relaxed = early[-1]

    (on,) = call(pass_kernel, "pass", [four], relaxed, initial)
    arrived = shifted(on, 1, 0)
    (change,) = call(change_kernel, "change", [both], arrived, mid, relaxed, guess)
    start_lo, start_hi = low, high
    late = []
    change_lo = change_hi = None
    for section in range(CF):
        state_lo, state_hi = shifted(change, 0, 1), shifted(change, 0, -1)
        if section == 0:
            change_lo, change_hi = state_lo, state_hi
        (change,) = call(
            late_kernel, f"late{section}", [both], change, state_lo, state_hi, coef, scratch=scratch_of(2)
        )
        late.append(change)
    (fine_state,) = call(fine_kernel, "fine", [forcing.shape], *early, *late[: CF - 1])

    state_lo, state_hi = shifted(change[0], 0, 1), shifted(change[0], 0, -1)
    last, on = call(
        last_kernel, "last", [four, four], change, state_lo, state_hi, relaxed, coef, scratch=scratch_of(1)
    )
    low, mid, high = shifted(on, 1, 1), shifted(on, 1, 0), shifted(on, 1, -1)
    moved, again, third = call(
        again_kernel, "again", [four] * 3, low, mid, high, start_lo, start_hi, change_lo, change_hi,
        arrived, change, relaxed, coef, scratch=scratch_of(2),
    )
    state_lo, state_hi = shifted(moved, 0, 1), shifted(moved, 0, -1)
    coarse_state, coarse_source = call(
        source_kernel, "source", [(2,) + initial.shape, (1,) + initial.shape], moved, state_lo, state_hi, last, again,
        third, coef, scratch=scratch_of(1),
    )
    return (fine_state, coarse_state, coarse_source)


def solution(mesh):
    return jax.shard_map(
        on_device,
        mesh=mesh,
        in_specs=(
            P("tm", "space", None, None),
            P("tm", "space", None, None),
            P("space", None, None),
            P("space", None, None),
            P(None, "space", None, None),
        ),
        out_specs=(
            P("tm", "space", None, None),
            P("tm", "space", None, None),
            P("tm", "space", None, None),
        ),
        check_vma=False,
    )
```

```python
import jax
import jax.numpy as jnp
from jax import lax
from jax.experimental import pallas as pl
from jax.experimental.pallas import tpu as pltpu
from jax.sharding import PartitionSpec as P

CF = 4
SLAB = 4
EDGE = SLAB - 1
ROWS = 4

storage_rate = 2.0


def shifted(value, dt, ds):
    times = lax.axis_size("tm")
    slabs = lax.axis_size("space")
    pairs = [
        (t * slabs + s, ((t + dt) % times) * slabs + (s + ds) % slabs)
        for t in range(times)
        for s in range(slabs)
    ]
    return lax.ppermute(value, ("tm", "space"), pairs)


def call(kernel, name, outs, *args, scratch=(), anywhere=0):
    held = [a if i < anywhere else pltpu.with_memory_space_constraint(a, pltpu.VMEM) for i, a in enumerate(args)]
    inside = pl.BlockSpec(memory_space=pltpu.VMEM)
    outside = pl.BlockSpec(memory_space=pl.ANY)
    return pl.pallas_call(
        kernel,
        out_shape=[pltpu.VMEM(shape, jnp.float32) for shape in outs],
        in_specs=[outside if i < anywhere else inside for i in range(len(args))],
        out_specs=[inside] * len(outs),
        scratch_shapes=[pltpu.VMEM(s, jnp.float32) if isinstance(s, tuple) else s for s in scratch],
        name=name,
        compiler_params=pltpu.CompilerParams(vmem_limit_bytes=16 * 2**20),
    )(*held)


PLANE = (ROWS, 8, 128)


def plane_of(ref, *at):
    return [ref[(*at, pl.ds(j, 8, stride=ROWS), slice(None))] for j in range(ROWS)]


def put_plane(ref, at, rows):
    for j in range(ROWS):
        ref[(*at, pl.ds(j, 8, stride=ROWS), slice(None))] = rows[j]


def x_lower(v):
    return pltpu.roll(v, 1, 1)


def x_upper(v):
    return pltpu.roll(v, 127, 1)


def y_lower(rows):
    return [pltpu.roll(rows[-1], 1, 0)] + rows[:-1]


def y_upper(rows):
    return rows[1:] + [pltpu.roll(rows[0], 7, 0)]


def rows_at(ref, *at):
    return [ref[(*at, j)] for j in range(ROWS)]


def put_rows(ref, at, rows):
    for j in range(ROWS):
        ref[(*at, j)] = rows[j]


WEST, EAST, SOUTH, NORTH, BELOW, ABOVE, STORAGE, FINE, COARSE, COARSEST = range(10)
REACH = SLAB + 2 * EDGE
FACTORS = {FINE: 1.0, COARSE: 1.0 / CF, COARSEST: 1.0 / (2 * CF)}


def step(coef, levels, window, source, put, near, far, right):
    count = len(levels)
    for turn in range(4):
        planes = REACH - 2 * turn
        out = [near, far, near, None][turn]
        held = [None, near, far, near][turn]
        for p in range(planes):
            at = p + turn
            links = [rows_at(coef, kind, at) for kind in range(6)]
            inverses = {level: rows_at(coef, level, at) for level in set(levels)}
            for b in range(count):
                if turn == 0:
                    lower, middle, upper = window(b, p), window(b, p + 1), window(b, p + 2)
                    stored = rows_at(coef, STORAGE, at)
                    factor = FACTORS[levels[b]]
                    if factor != 1.0:
                        stored = [s * factor for s in stored]
                    rhs = [s * v for s, v in zip(stored, middle)]
                    if source is not None:
                        rhs = [r + f for r, f in zip(rhs, source(b, p))]
                    if 0 < p < planes - 1:
                        put_rows(right, (b, p - 1), rhs)
                else:
                    lower, middle, upper = [rows_at(held, b, p + k) for k in range(3)]
                    rhs = rows_at(right, b, at - 1)
                south_of, north_of = y_lower(middle), y_upper(middle)
                result = []
                for j in range(ROWS):
                    west, east, south, north, below, above = [link[j] for link in links]
                    total = rhs[j] + (west * x_lower(middle[j]) + east * x_upper(middle[j]))
                    total = total + (south * south_of[j] + north * north_of[j])
                    total = total + (below * lower[j] + above * upper[j])
                    result.append(total * inverses[levels[b]][j])
                if out is None:
                    put(b, p, result)
                else:
                    put_rows(out, (b, p), result)


def scratch_of(count):
    return [(count, 10) + PLANE, (count, 8) + PLANE, (count, 8) + PLANE]


def windows(lo, own, hi):
    def window(b, p):
        if p < SLAB:
            return rows_at(lo, b, p)
        if p < 2 * SLAB:
            return rows_at(own, b, p - SLAB)
        return rows_at(hi, b, p - 2 * SLAB)

    return window


UP_START, UP_FORCE, UP_FIELD = 0, 8, 14
MESSAGE = 30
X, Y, Z, PORE = range(4)


def prepare_kernel(
    forcing, guess, porosity, permeability, up, down, up_later, down_later, force, start, field,
    force_in, guess_in, pore_in, perm_in, arrivals,
):
    copies = [
        pltpu.make_async_copy(source, target, arrivals.at[i])
        for i, (source, target) in enumerate(
            ((guess.at[0], guess_in), (porosity, pore_in), (permeability, perm_in), (forcing, force_in))
        )
    ]
    for copy in copies:
        copy.start()
    for copy in copies[:3]:
        copy.wait()
    for z in range(SLAB):
        rows = plane_of(guess_in, z)
        put_rows(start, (z,), rows)
        for target in (up, down):
            put_rows(target, (UP_START + SLAB + z,), rows)
        for kind in range(4):
            rows = plane_of(pore_in, z) if kind == PORE else plane_of(perm_in, kind, z)
            put_rows(field, (kind, z), rows)
            for target in (up, down):
                put_rows(target, (UP_FIELD + SLAB * kind + z,), rows)
    copies[3].wait()
    for z in range(SLAB):
        for b in range(2):
            for i in range(CF):
                rows = plane_of(force_in, b * CF + i, z)
                put_rows(force, (b, i, z), rows)
                for target, later, skip in ((up, up_later, 1), (down, down_later, 0)):
                    if 0 <= z - skip < EDGE:
                        if i == 0:
                            put_rows(target, (UP_FORCE + EDGE * b + z - skip,), rows)
                        else:
                            put_rows(later, (b, i - 1, z - skip), rows)


def complete_kernel(arrived, guess, up_part, down_part, up, down, start):
    for z in range(SLAB):
        rows = plane_of(arrived, z)
        put_rows(start, (0, z), rows)
        put_rows(start, (1, z), rows_at(guess, z))
        put_rows(up, (UP_START + z,), rows)
        put_rows(down, (UP_START + z,), rows)
    up[SLAB:] = up_part[SLAB:]
    down[SLAB:] = down_part[SLAB:]


def harmonic(lower, upper):
    return [2.0 * a * b / (a + b) for a, b in zip(lower, upper)]


def face_terms(held):
    column = lax.broadcasted_iota(jnp.int32, (8, 128), 1)
    row = lax.broadcasted_iota(jnp.int32, (8, 128), 0)
    zero = jnp.zeros((8, 128), jnp.float32)
    kx, ky, kz = [held(kind, 0) for kind in (X, Y, Z)]
    side = harmonic(kx, [x_upper(k) for k in kx])
    east_link = [jnp.where(column == 127, zero, v) for v in side]
    east = [jnp.where(column == 127, k, v) for k, v in zip(kx, side)]
    side = [x_lower(v) for v in side]
    west_link = [jnp.where(column == 0, zero, v) for v in side]
    west = [jnp.where(column == 0, k, v) for k, v in zip(kx, side)]
    side = harmonic(ky, y_upper(ky))
    north_link, north = list(side), list(side)
    north_link[-1] = jnp.where(row == 7, zero, side[-1])
    north[-1] = jnp.where(row == 7, ky[-1], side[-1])
    side = y_lower(side)
    south_link, south = list(side), list(side)
    south_link[0] = jnp.where(row == 0, zero, side[0])
    south[0] = jnp.where(row == 0, ky[0], side[0])
    links = [west_link, east_link, south_link, north_link]
    return links, [west, east, south, north], kz


def put_coefficients(coef, p, height, held, levels):
    last = SLAB * lax.axis_size("space") - 1
    zero = jnp.zeros((8, 128), jnp.float32)
    links, sides, kz = face_terms(held)
    below = harmonic(held(Z, -1), kz)
    above = harmonic(kz, held(Z, 1))
    floor, top = height == 0, height == last
    links.append([jnp.where(floor, zero, v) for v in below])
    links.append([jnp.where(top, zero, v) for v in above])
    below = [jnp.where(floor, k, v) for k, v in zip(kz, below)]
    above = [jnp.where(top, k, v) for k, v in zip(kz, above)]
    west, east, south, north = sides
    for kind, rows in enumerate(links):
        put_rows(coef, (kind, p), rows)
    stored = [storage_rate * v for v in held(PORE, 0)]
    put_rows(coef, (STORAGE, p), stored)
    for j in range(ROWS):
        coupling = ((west[j] + east[j]) + (south[j] + north[j])) + (below[j] + above[j])
        for level in levels:
            coef[level, p, j] = 1.0 / (stored[j] * FACTORS[level] + coupling)


def first_kernel(start, lo, hi, force, field, coef, state, near, far, right):
    position = lax.axis_index("space")
    cells = SLAB * lax.axis_size("space")
    for p in range(REACH):

        def held(kind, k, p=p):
            part, at = divmod(p + 1 + k, SLAB)
            if part == 1:
                return rows_at(field, kind, at)
            return rows_at([lo, None, hi][part], UP_FIELD + SLAB * kind + at)

        height = lax.rem(position * SLAB + p - EDGE + cells, cells)
        put_coefficients(coef, p, height, held, (FINE,))

    def window(b, p):
        part, at = divmod(p, SLAB)
        if part == 1:
            return rows_at(start, b, at)
        return rows_at([lo, None, hi][part], UP_START + SLAB * b + at)

    def source(b, p):
        if p < EDGE:
            return rows_at(lo, UP_FORCE + EDGE * b + p)
        if p < EDGE + SLAB:
            return rows_at(force, b, 0, p - EDGE)
        return rows_at(hi, UP_FORCE + EDGE * b + p - EDGE - SLAB)

    step(coef, [FINE, FINE], window, source, lambda b, p, rows: put_rows(state, (b, p), rows), near, far, right)


def early_kernel(section):
    def kernel(own, lo, hi, force, force_lo, force_hi, coef, field, state, kept, near, far, right):
        kept[...] = field[...]

        def source(b, p):
            if p < EDGE:
                return rows_at(force_lo, b, section - 1, p)
            if p < EDGE + SLAB:
                return rows_at(force, b, section, p - EDGE)
            return rows_at(force_hi, b, section - 1, p - EDGE - SLAB)

        put = lambda b, p, rows: put_rows(state, (b, p), rows)
        step(coef, [FINE, FINE], windows(lo, own, hi), source, put, near, far, right)

    return kernel


def pass_kernel(relaxed, initial, on):
    last_time = lax.axis_index("tm") == lax.axis_size("tm") - 1
    for z in range(SLAB):
        rows = [jnp.where(last_time, a, b) for a, b in zip(plane_of(initial, z), rows_at(relaxed, 1, z))]
        put_rows(on, (z,), rows)


def change_kernel(arrived, relaxed, start, change):
    for z in range(SLAB):
        for j in range(ROWS):
            change[0, z, j] = arrived[z, j] - start[0, z, j]
            change[1, z, j] = relaxed[0, z, j] - start[1, z, j]


HALO = 24
SPAN = 2 * HALO + SLAB
PACK = 16
INNER = 8


def pack_kernel(own, lo, hi, lo_two, hi_two, up, down):
    for k in range(own.shape[0]):
        for z in range(SLAB):
            for j in range(ROWS):
                parts = [lo_two[k, z, j], lo[k, z, j], own[k, z, j], hi[k, z, j], hi_two[k, z, j]]
                for i in range(4):
                    up[k, SLAB * i + z, j] = parts[i]
                    down[k, SLAB * i + z, j] = parts[i + 1]


def pack_field_kernel(own, lo, hi, lo_two, hi_two, up, down):
    for k in range(4):
        for z in range(SLAB):
            at = UP_FIELD + SLAB * k + z
            for j in range(ROWS):
                parts = [lo_two[k, z, j], lo[at, j], own[k, z, j], hi[at, j], hi_two[k, z, j]]
                for i in range(4):
                    up[k, SLAB * i + z, j] = parts[i]
                    down[k, SLAB * i + z, j] = parts[i + 1]


def wide_kernel(own, lo, hi, lo_two, hi_two, lo_far, hi_far, coef, wide):
    def fill(target, z, part, at):
        for k in range(4):
            put_rows(wide, (k, target + z), rows_at(part, *at(k)))

    for z in range(PACK):
        fill(0, z, lo_far, lambda k: (k, z))
        fill(HALO + 3 * SLAB, z, hi_far, lambda k: (k, z))
    for z in range(SLAB):
        fill(HALO - 2 * SLAB, z, lo_two, lambda k: (k, z))
        fill(HALO - SLAB, z, lo, lambda k: (UP_FIELD + SLAB * k + z,))
        fill(HALO, z, own, lambda k: (k, z))
        fill(HALO + SLAB, z, hi, lambda k: (UP_FIELD + SLAB * k + z,))
        fill(HALO + 2 * SLAB, z, hi_two, lambda k: (k, z))
    position = lax.axis_index("space")
    cells = SLAB * lax.axis_size("space")

    def body(start, size):
        for k in range(size):
            p = start + k
            height = lax.rem(position * SLAB + p + (cells - HALO + 1), cells)
            held = lambda kind, i, p=p: rows_at(wide, kind, p + 1 + i)
            put_coefficients(coef, p, height, held, (FINE, COARSE, COARSEST))

    in_chunks(SPAN - 2, 10, body)


CHUNK = 26


def in_chunks(count, chunk, body):
    pieces = max(1, round(count / chunk))
    size = -(-count // pieces)
    if pieces == 1:
        body(0, size)
        return

    def turn(i, carry):
        body(jnp.minimum(i * size, count - size), size)
        return carry

    lax.fori_loop(0, pieces, turn, 0)


def sweep_planes(coef, level, blocks, old, new, right, low, high, shift, first):
    factor = FACTORS[level]

    def body(start, size):
        for k in range(size):
            w = low + start + k
            at = w + shift
            links = [rows_at(coef, kind, at) for kind in range(6)]
            inverse = rows_at(coef, level, at)
            if first:
                stored = rows_at(coef, STORAGE, at)
                if factor != 1.0:
                    stored = [s * factor for s in stored]
            for b in blocks:
                lower, middle, upper = [rows_at(old, b, w + i) for i in (-1, 0, 1)]
                if first:
                    rhs = [s * v for s, v in zip(stored, middle)]
                    put_rows(right, (b, w), rhs)
                else:
                    rhs = rows_at(right, b, w)
                south_of, north_of = y_lower(middle), y_upper(middle)
                for j in range(ROWS):
                    west, east, south, north, below, above = [link[j] for link in links]
                    total = rhs[j] + (west * x_lower(middle[j]) + east * x_upper(middle[j]))
                    total = total + (south * south_of[j] + north * north_of[j])
                    total = total + (below * lower[j] + above * upper[j])
                    new[b, w, j] = total * inverse[j]

    in_chunks(high - low, CHUNK * 2 // len(blocks), body)


def wide_step(coef, level, blocks, near, far, right, low, high, shift):
    for turn in range(4):
        old, new = (near, far) if turn % 2 == 0 else (far, near)
        sweep_planes(coef, level, blocks, old, new, right, low + turn + 1, high - turn - 1, shift, turn == 0)


def late_kernel(
    own, lo, hi, lo_two, hi_two, lo_far, hi_far, relaxed, coef, late0, late1, late2, change, last, on, near, far, right
):
    last_time = lax.axis_index("tm") == lax.axis_size("tm") - 1
    for b in range(2):
        for z in range(PACK):
            put_rows(near, (b, z), rows_at(lo_far, b, z))
            put_rows(near, (b, HALO + 3 * SLAB + z), rows_at(hi_far, b, z))
        for i, part in enumerate((lo_two, lo, own, hi, hi_two)):
            for z in range(SLAB):
                put_rows(near, (b, HALO + SLAB * (i - 2) + z), rows_at(part, b, z))
    for section, late in enumerate((late0, late1, late2, change)):
        wide_step(coef, FINE, (0, 1), near, far, right, SLAB * section, SPAN - SLAB * section, -1)
        for b in range(2):
            for z in range(SLAB):
                put_rows(late, (b, z), rows_at(near, b, HALO + z))
    wide_step(coef, COARSE, (0,), near, far, right, HALO - INNER, HALO + SLAB + INNER, -1)
    for z in range(3 * SLAB):
        w = HALO - SLAB + z
        rows = [a + d for a, d in zip(rows_at(near, 1, w), rows_at(near, 0, w))]
        put_rows(on, (z,), [jnp.where(last_time, 0.0, d) for d in rows])
        if SLAB <= z < 2 * SLAB:
            put_rows(last, (z - SLAB,), [u + d for u, d in zip(rows_at(relaxed, 1, z - SLAB), rows)])


def fine_kernel(early0, early1, early2, relaxed, late0, late1, late2, fine):
    for b in range(2):
        for z in range(SLAB):
            for i, (early, late) in enumerate(((early0, late0), (early1, late1), (early2, late2))):
                rows = [u + d for u, d in zip(rows_at(early, b, z), rows_at(late, b, z))]
                put_plane(fine, (b * CF + i, z), rows)
            put_plane(fine, (b * CF + CF - 1, z), rows_at(relaxed, b, z))


def coarse_kernel(
    below, above, arrived, lo, hi, change_lo, change_hi, change, relaxed, last, coef, state, source, near, far, right
):
    for z in range(3 * SLAB):
        put_rows(near, (0, z), rows_at(below, z))
        if z >= SLAB:
            put_rows(near, (0, INNER + z), rows_at(above, z))
    for z in range(3 * SLAB):
        part, at = divmod(z, SLAB)
        if part == 1:
            rows = rows_at(arrived, at)
        else:
            halo, moved = (lo, change_lo) if part == 0 else (hi, change_hi)
            rows = [u + d for u, d in zip(rows_at(halo, UP_START + at), rows_at(moved, 0, at))]
        put_rows(near, (1, SLAB + z), [u + d for u, d in zip(rows, rows_at(near, 0, SLAB + z))])
    shift = HALO - INNER - 1
    wide_step(coef, COARSE, (0,), near, far, right, 0, SLAB + 2 * INNER, shift)
    for z in range(SLAB):
        point = [u + d for u, d in zip(rows_at(relaxed, 0, z), rows_at(change, 0, z))]
        put_plane(state, (0, z), [u + d for u, d in zip(point, rows_at(near, 0, INNER + z))])
        put_plane(state, (1, z), rows_at(last, z))
    wide_step(coef, COARSE, (0,), near, far, right, SLAB, SLAB + 3 * SLAB, shift)
    wide_step(coef, COARSEST, (1,), near, far, right, SLAB, SLAB + 3 * SLAB, shift)
    for z in range(SLAB):
        both = zip(rows_at(near, 0, INNER + z), rows_at(last, z), rows_at(near, 1, INNER + z))
        put_plane(source, (0, z), [(d + u) - w for d, u, w in both])


def on_device(forcing, c_guess, initial, porosity, permeability):
    four = (SLAB,) + PLANE
    both = (2,) + four
    last_time = lax.axis_index("tm") == lax.axis_size("tm") - 1

    arrived = shifted(jnp.where(last_time, initial, c_guess[1]), 1, 0)
    later = (2, CF - 1, EDGE) + PLANE
    message = (MESSAGE,) + PLANE
    up, down, up_later, down_later, force, guess, field = call(
        prepare_kernel, "prepare", [message, message, later, later, (2, CF) + four, four, (4,) + four],
        forcing, c_guess, porosity, permeability, anywhere=4,
        scratch=[forcing.shape, initial.shape, porosity.shape, permeability.shape, pltpu.SemaphoreType.DMA((4,))],
    )
    up, down, start = call(complete_kernel, "complete", [message, message, both], arrived, guess, up, down)
    lo, hi = shifted(up, 0, 1), shifted(down, 0, -1)
    force_lo, force_hi = shifted(up_later, 0, 1), shifted(down_later, 0, -1)
    coef, state = call(
        first_kernel, "first", [(8, REACH) + PLANE, both], start, lo, hi, force, field, scratch=scratch_of(2)
    )
    early = [state]
    for section in range(1, CF):
        state_lo, state_hi = shifted(state, 0, 1), shifted(state, 0, -1)
        state, kept = call(
            early_kernel(section), f"early{section}", [both, (4,) + four], state, state_lo, state_hi, force,
            force_lo, force_hi, coef, field, scratch=scratch_of(2),
        )
        early.append(state)
        if section == 1:
            field_lo, field_hi = shifted(kept, 0, 2), shifted(kept, 0, -2)
            packed = (4, PACK) + PLANE
            field_up, field_down = call(
                pack_field_kernel, "pack_field", [packed, packed], kept, lo, hi, field_lo, field_hi
            )
            field_far_lo, field_far_hi = shifted(field_up, 0, 4), shifted(field_down, 0, -4)
    relaxed = early[-1]

    (on,) = call(pass_kernel, "pass", [four], relaxed, initial)
    arrived = shifted(on, 1, 0)
    (change,) = call(change_kernel, "change", [both], arrived, relaxed, start)
    change_lo, change_hi = shifted(change, 0, 1), shifted(change, 0, -1)
    two_lo, two_hi = shifted(change, 0, 2), shifted(change, 0, -2)
    packed = (2, PACK) + PLANE
    change_up, change_down = call(pack_kernel, "pack", [packed, packed], change, change_lo, change_hi, two_lo, two_hi)
    far_lo, far_hi = shifted(change_up, 0, 4), shifted(change_down, 0, -4)
    (coef,) = call(
        wide_kernel, "wide", [(10, SPAN - 2) + PLANE], field, lo, hi, field_lo, field_hi, field_far_lo, field_far_hi,
        scratch=[(4, SPAN) + PLANE],
    )
    late0, late1, late2, changed, last, on = call(
        late_kernel, "late", [both] * 4 + [four, (3 * SLAB,) + PLANE], change, change_lo, change_hi, two_lo, two_hi,
        far_lo, far_hi, relaxed, coef, scratch=[(2, SPAN) + PLANE] * 3,
    )
    below, above = shifted(on, 1, 1), shifted(on, 1, -1)
    (fine_state,) = call(fine_kernel, "fine", [forcing.shape], *early, late0, late1, late2)
    coarse_state, coarse_source = call(
        coarse_kernel, "coarse", [(2,) + initial.shape, (1,) + initial.shape], below, above, arrived, lo, hi,
        change_lo, change_hi, changed, relaxed, last, coef, scratch=[(2, SLAB + 2 * INNER) + PLANE] * 3,
    )
    return (fine_state, coarse_state, coarse_source)


def solution(mesh):
    return jax.shard_map(
        on_device,
        mesh=mesh,
        in_specs=(
            P("tm", "space", None, None),
            P("tm", "space", None, None),
            P("space", None, None),
            P("space", None, None),
            P(None, "space", None, None),
        ),
        out_specs=(
            P("tm", "space", None, None),
            P("tm", "space", None, None),
            P("tm", "space", None, None),
        ),
        check_vma=False,
    )
```

```python
import jax
import jax.numpy as jnp
from jax import lax
from jax.experimental import pallas as pl
from jax.experimental.pallas import tpu as pltpu
from jax.sharding import PartitionSpec as P

CF = 4
SLAB = 4
EDGE = SLAB - 1
ROWS = 4

storage_rate = 2.0


def shifted(value, dt, ds):
    times = lax.axis_size("tm")
    slabs = lax.axis_size("space")
    pairs = [
        (t * slabs + s, ((t + dt) % times) * slabs + (s + ds) % slabs)
        for t in range(times)
        for s in range(slabs)
    ]
    return lax.ppermute(value, ("tm", "space"), pairs)


def swapped(value):
    return lax.ppermute(value, "tm", [(t, t ^ 1) for t in range(lax.axis_size("tm"))])


def call(kernel, name, outs, *args, scratch=(), anywhere=0, stored=False):
    held = [
        pltpu.with_memory_space_constraint(a, pltpu.HBM if i < anywhere else pltpu.VMEM) for i, a in enumerate(args)
    ]
    inside = pl.BlockSpec(memory_space=pltpu.VMEM)
    outside = pl.BlockSpec(memory_space=pl.ANY)
    return pl.pallas_call(
        kernel,
        out_shape=[(pltpu.HBM if stored else pltpu.VMEM)(shape, jnp.float32) for shape in outs],
        in_specs=[outside if i < anywhere else inside for i in range(len(args))],
        out_specs=[outside if stored else inside] * len(outs),
        scratch_shapes=[pltpu.VMEM(s, jnp.float32) if isinstance(s, tuple) else s for s in scratch],
        name=name,
        compiler_params=pltpu.CompilerParams(vmem_limit_bytes=16 * 2**20),
    )(*held)


PLANE = (ROWS, 8, 128)


def plane_of(ref, *at):
    return [ref[(*at, pl.ds(j, 8, stride=ROWS), slice(None))] for j in range(ROWS)]


def put_plane(ref, at, rows):
    for j in range(ROWS):
        ref[(*at, pl.ds(j, 8, stride=ROWS), slice(None))] = rows[j]


def x_lower(v):
    return pltpu.roll(v, 1, 1)


def x_upper(v):
    return pltpu.roll(v, 127, 1)


def y_lower(rows):
    return [pltpu.roll(rows[-1], 1, 0)] + rows[:-1]


def y_upper(rows):
    return rows[1:] + [pltpu.roll(rows[0], 7, 0)]


def rows_at(ref, *at):
    return [ref[(*at, j)] for j in range(ROWS)]


def put_rows(ref, at, rows):
    for j in range(ROWS):
        ref[(*at, j)] = rows[j]


WEST, EAST, SOUTH, NORTH, BELOW, ABOVE, STORAGE, FINE, COARSE, COARSEST = range(10)
REACH = SLAB + 2 * EDGE
FACTORS = {FINE: 1.0, COARSE: 1.0 / CF, COARSEST: 1.0 / (2 * CF)}


def step(coef, levels, window, source, put, near, far, right):
    count = len(levels)
    for turn in range(4):
        planes = REACH - 2 * turn
        out = [near, far, near, None][turn]
        held = [None, near, far, near][turn]
        for p in range(planes):
            at = p + turn
            links = [rows_at(coef, kind, at) for kind in range(6)]
            inverses = {level: rows_at(coef, level, at) for level in set(levels)}
            for b in range(count):
                if turn == 0:
                    lower, middle, upper = window(b, p), window(b, p + 1), window(b, p + 2)
                    stored = rows_at(coef, STORAGE, at)
                    factor = FACTORS[levels[b]]
                    if factor != 1.0:
                        stored = [s * factor for s in stored]
                    rhs = [s * v for s, v in zip(stored, middle)]
                    if source is not None:
                        rhs = [r + f for r, f in zip(rhs, source(b, p))]
                    if 0 < p < planes - 1:
                        put_rows(right, (b, p - 1), rhs)
                else:
                    lower, middle, upper = [rows_at(held, b, p + k) for k in range(3)]
                    rhs = rows_at(right, b, at - 1)
                south_of, north_of = y_lower(middle), y_upper(middle)
                result = []
                for j in range(ROWS):
                    west, east, south, north, below, above = [link[j] for link in links]
                    total = rhs[j] + (west * x_lower(middle[j]) + east * x_upper(middle[j]))
                    total = total + (south * south_of[j] + north * north_of[j])
                    total = total + (below * lower[j] + above * upper[j])
                    result.append(total * inverses[levels[b]][j])
                if out is None:
                    put(b, p, result)
                else:
                    put_rows(out, (b, p), result)


def scratch_of(count):
    return [(count, 10) + PLANE, (count, 8) + PLANE, (count, 8) + PLANE]


def windows(lo, own, hi):
    def window(b, p):
        if p < SLAB:
            return rows_at(lo, b, p)
        if p < 2 * SLAB:
            return rows_at(own, b, p - SLAB)
        return rows_at(hi, b, p - 2 * SLAB)

    return window


UP_START, UP_FORCE, UP_FIELD = 0, 8, 14
MESSAGE = 30
X, Y, Z, PORE = range(4)


def own_half(first, second):
    even = lax.rem(lax.axis_index("tm"), 2) == 0
    return [jnp.where(even, a, b) for a, b in zip(first, second)]


def prepare_kernel(
    forcing, guess, porosity, permeability, up, down, up_later, down_later, force, start, field, half,
    force_in, guess_in, pore_in, perm_in, arrivals,
):
    copies = [
        pltpu.make_async_copy(source, target, arrivals.at[i])
        for i, (source, target) in enumerate(
            ((guess.at[0], guess_in), (porosity, pore_in), (permeability, perm_in), (forcing, force_in))
        )
    ]
    for copy in copies:
        copy.start()
    for copy in copies[:3]:
        copy.wait()
    for z in range(SLAB):
        rows = plane_of(guess_in, z)
        put_rows(start, (z,), rows)
        for target in (up, down):
            put_rows(target, (UP_START + SLAB + z,), rows)
        for kind in range(4):
            rows = plane_of(pore_in, z) if kind == PORE else plane_of(perm_in, kind, z)
            put_rows(field, (kind, z), rows)
            for target in (up, down):
                put_rows(target, (UP_FIELD + SLAB * kind + z,), rows)
        for kind in range(2):
            put_rows(half, (kind, z), own_half(rows_at(field, kind, z), rows_at(field, kind + 2, z)))
    copies[3].wait()
    for z in range(SLAB):
        for b in range(2):
            for i in range(CF):
                rows = plane_of(force_in, b * CF + i, z)
                put_rows(force, (b, i, z), rows)
                for target, later, skip in ((up, up_later, 1), (down, down_later, 0)):
                    if 0 <= z - skip < EDGE:
                        if i == 0:
                            put_rows(target, (UP_FORCE + EDGE * b + z - skip,), rows)
                        else:
                            put_rows(later, (b, i - 1, z - skip), rows)


def complete_kernel(arrived, guess, up_part, down_part, up, down, start):
    for z in range(SLAB):
        rows = plane_of(arrived, z)
        put_rows(start, (0, z), rows)
        put_rows(start, (1, z), rows_at(guess, z))
        put_rows(up, (UP_START + z,), rows)
        put_rows(down, (UP_START + z,), rows)
    up[SLAB:] = up_part[SLAB:]
    down[SLAB:] = down_part[SLAB:]


def harmonic(lower, upper):
    return [2.0 * a * b / (a + b) for a, b in zip(lower, upper)]


def face_terms(held):
    column = lax.broadcasted_iota(jnp.int32, (8, 128), 1)
    row = lax.broadcasted_iota(jnp.int32, (8, 128), 0)
    zero = jnp.zeros((8, 128), jnp.float32)
    kx, ky, kz = [held(kind, 0) for kind in (X, Y, Z)]
    side = harmonic(kx, [x_upper(k) for k in kx])
    east_link = [jnp.where(column == 127, zero, v) for v in side]
    east = [jnp.where(column == 127, k, v) for k, v in zip(kx, side)]
    side = [x_lower(v) for v in side]
    west_link = [jnp.where(column == 0, zero, v) for v in side]
    west = [jnp.where(column == 0, k, v) for k, v in zip(kx, side)]
    side = harmonic(ky, y_upper(ky))
    north_link, north = list(side), list(side)
    north_link[-1] = jnp.where(row == 7, zero, side[-1])
    north[-1] = jnp.where(row == 7, ky[-1], side[-1])
    side = y_lower(side)
    south_link, south = list(side), list(side)
    south_link[0] = jnp.where(row == 0, zero, side[0])
    south[0] = jnp.where(row == 0, ky[0], side[0])
    links = [west_link, east_link, south_link, north_link]
    return links, [west, east, south, north], kz


def put_coefficients(coef, p, height, held, levels):
    last = SLAB * lax.axis_size("space") - 1
    zero = jnp.zeros((8, 128), jnp.float32)
    links, sides, kz = face_terms(held)
    below = harmonic(held(Z, -1), kz)
    above = harmonic(kz, held(Z, 1))
    floor, top = height == 0, height == last
    links.append([jnp.where(floor, zero, v) for v in below])
    links.append([jnp.where(top, zero, v) for v in above])
    below = [jnp.where(floor, k, v) for k, v in zip(kz, below)]
    above = [jnp.where(top, k, v) for k, v in zip(kz, above)]
    west, east, south, north = sides
    for kind, rows in enumerate(links):
        put_rows(coef, (kind, p), rows)
    stored = [storage_rate * v for v in held(PORE, 0)]
    put_rows(coef, (STORAGE, p), stored)
    for j in range(ROWS):
        coupling = ((west[j] + east[j]) + (south[j] + north[j])) + (below[j] + above[j])
        for level in levels:
            coef[level, p, j] = 1.0 / (stored[j] * FACTORS[level] + coupling)


def first_kernel(start, lo, hi, force, field, coef, state, near, far, right):
    position = lax.axis_index("space")
    cells = SLAB * lax.axis_size("space")
    for p in range(REACH):

        def held(kind, k, p=p):
            part, at = divmod(p + 1 + k, SLAB)
            if part == 1:
                return rows_at(field, kind, at)
            return rows_at([lo, None, hi][part], UP_FIELD + SLAB * kind + at)

        height = lax.rem(position * SLAB + p - EDGE + cells, cells)
        put_coefficients(coef, p, height, held, (FINE,))

    def window(b, p):
        part, at = divmod(p, SLAB)
        if part == 1:
            return rows_at(start, b, at)
        return rows_at([lo, None, hi][part], UP_START + SLAB * b + at)

    def source(b, p):
        if p < EDGE:
            return rows_at(lo, UP_FORCE + EDGE * b + p)
        if p < EDGE + SLAB:
            return rows_at(force, b, 0, p - EDGE)
        return rows_at(hi, UP_FORCE + EDGE * b + p - EDGE - SLAB)

    step(coef, [FINE, FINE], window, source, lambda b, p, rows: put_rows(state, (b, p), rows), near, far, right)


def early_kernel(section):
    def kernel(own, lo, hi, force, force_lo, force_hi, coef, state, near, far, right):
        def source(b, p):
            if p < EDGE:
                return rows_at(force_lo, b, section - 1, p)
            if p < EDGE + SLAB:
                return rows_at(force, b, section, p - EDGE)
            return rows_at(force_hi, b, section - 1, p - EDGE - SLAB)

        put = lambda b, p, rows: put_rows(state, (b, p), rows)
        step(coef, [FINE, FINE], windows(lo, own, hi), source, put, near, far, right)

    return kernel


def pass_kernel(relaxed, initial, on):
    last_time = lax.axis_index("tm") == lax.axis_size("tm") - 1
    for z in range(SLAB):
        rows = [jnp.where(last_time, a, b) for a, b in zip(plane_of(initial, z), rows_at(relaxed, 1, z))]
        put_rows(on, (z,), rows)


def change_kernel(arrived, relaxed, start, change):
    for z in range(SLAB):
        for j in range(ROWS):
            change[0, z, j] = arrived[z, j] - start[0, z, j]
            change[1, z, j] = relaxed[0, z, j] - start[1, z, j]


HALO = 24
SPAN = 2 * HALO + SLAB
PACK = 16
INNER = 8


def pack_kernel(own, lo, hi, lo_two, hi_two, up, down):
    for k in range(own.shape[0]):
        for z in range(SLAB):
            for j in range(ROWS):
                parts = [lo_two[k, z, j], lo[k, z, j], own[k, z, j], hi[k, z, j], hi_two[k, z, j]]
                for i in range(4):
                    up[k, SLAB * i + z, j] = parts[i]
                    down[k, SLAB * i + z, j] = parts[i + 1]


def pack_field_kernel(own, lo, hi, lo_two, hi_two, after, up, down):
    for k in range(2):
        for z in range(SLAB):
            at = UP_FIELD + SLAB * k + z
            near_lo = own_half(rows_at(lo, at), rows_at(lo, at + 2 * SLAB))
            near_hi = own_half(rows_at(hi, at), rows_at(hi, at + 2 * SLAB))
            parts = [rows_at(lo_two, k, z), near_lo, rows_at(own, k, z), near_hi, rows_at(hi_two, k, z)]
            for i in range(4):
                put_rows(up, (k, SLAB * i + z), parts[i])
                put_rows(down, (k, SLAB * i + z), parts[i + 1])


def share_kernel(lo_two, hi_two, lo_far, hi_far, after, share):
    share[:, :PACK] = lo_far[...]
    share[:, PACK : PACK + SLAB] = lo_two[...]
    share[:, PACK + SLAB : PACK + 2 * SLAB] = hi_two[...]
    share[:, PACK + 2 * SLAB :] = hi_far[...]


def wide_kernel(own, lo, hi, mine, other, coef, wide):
    for k in range(2):
        for z in range(PACK + SLAB):
            for at, target in ((z, z), (PACK + SLAB + z, HALO + 2 * SLAB + z)):
                a, b = rows_at(mine, k, at), rows_at(other, k, at)
                put_rows(wide, (k, target), own_half(a, b))
                put_rows(wide, (k + 2, target), own_half(b, a))
    for k in range(4):
        for z in range(SLAB):
            at = UP_FIELD + SLAB * k + z
            put_rows(wide, (k, HALO - SLAB + z), rows_at(lo, at))
            put_rows(wide, (k, HALO + z), rows_at(own, k, z))
            put_rows(wide, (k, HALO + SLAB + z), rows_at(hi, at))
    position = lax.axis_index("space")
    cells = SLAB * lax.axis_size("space")

    def body(start, size):
        for k in range(size):
            p = start + k
            height = lax.rem(position * SLAB + p + (cells - HALO + 1), cells)
            held = lambda kind, i, p=p: rows_at(wide, kind, p + 1 + i)
            put_coefficients(coef, p, height, held, (FINE, COARSE, COARSEST))

    in_chunks(SPAN - 2, 10, body)


CHUNK = 26


def in_chunks(count, chunk, body):
    pieces = max(1, round(count / chunk))
    size = -(-count // pieces)
    if pieces == 1:
        body(0, size)
        return

    def turn(i, carry):
        body(jnp.minimum(i * size, count - size), size)
        return carry

    lax.fori_loop(0, pieces, turn, 0)


def sweep_planes(coef, level, blocks, old, new, right, low, high, shift, first):
    factor = FACTORS[level]

    def body(start, size):
        for k in range(size):
            w = low + start + k
            at = w + shift
            links = [rows_at(coef, kind, at) for kind in range(6)]
            inverse = rows_at(coef, level, at)
            if first:
                stored = rows_at(coef, STORAGE, at)
                if factor != 1.0:
                    stored = [s * factor for s in stored]
            for b in blocks:
                lower, middle, upper = [rows_at(old, b, w + i) for i in (-1, 0, 1)]
                if first:
                    rhs = [s * v for s, v in zip(stored, middle)]
                    put_rows(right, (b, w), rhs)
                else:
                    rhs = rows_at(right, b, w)
                south_of, north_of = y_lower(middle), y_upper(middle)
                for j in range(ROWS):
                    west, east, south, north, below, above = [link[j] for link in links]
                    total = rhs[j] + (west * x_lower(middle[j]) + east * x_upper(middle[j]))
                    total = total + (south * south_of[j] + north * north_of[j])
                    total = total + (below * lower[j] + above * upper[j])
                    new[b, w, j] = total * inverse[j]

    in_chunks(high - low, CHUNK * 2 // len(blocks), body)


def wide_step(coef, level, blocks, near, far, right, low, high, shift):
    for turn in range(4):
        old, new = (near, far) if turn % 2 == 0 else (far, near)
        sweep_planes(coef, level, blocks, old, new, right, low + turn + 1, high - turn - 1, shift, turn == 0)


def late_kernel(
    own, lo, hi, lo_two, hi_two, lo_far, hi_far, relaxed, coef, late0, late1, late2, change, last, on, near, far, right
):
    last_time = lax.axis_index("tm") == lax.axis_size("tm") - 1
    for b in range(2):
        for z in range(PACK):
            put_rows(near, (b, z), rows_at(lo_far, b, z))
            put_rows(near, (b, HALO + 3 * SLAB + z), rows_at(hi_far, b, z))
        for i, part in enumerate((lo_two, lo, own, hi, hi_two)):
            for z in range(SLAB):
                put_rows(near, (b, HALO + SLAB * (i - 2) + z), rows_at(part, b, z))
    for section, late in enumerate((late0, late1, late2, change)):
        wide_step(coef, FINE, (0, 1), near, far, right, SLAB * section, SPAN - SLAB * section, -1)
        for b in range(2):
            for z in range(SLAB):
                put_rows(late, (b, z), rows_at(near, b, HALO + z))
    wide_step(coef, COARSE, (0,), near, far, right, HALO - INNER, HALO + SLAB + INNER, -1)
    for z in range(3 * SLAB):
        w = HALO - SLAB + z
        rows = [a + d for a, d in zip(rows_at(near, 1, w), rows_at(near, 0, w))]
        put_rows(on, (z,), [jnp.where(last_time, 0.0, d) for d in rows])
        if SLAB <= z < 2 * SLAB:
            put_rows(last, (z - SLAB,), [u + d for u, d in zip(rows_at(relaxed, 1, z - SLAB), rows)])


def fine_kernel(early0, early1, early2, relaxed, late0, late1, late2, fine):
    for b in range(2):
        for z in range(SLAB):
            for i, (early, late) in enumerate(((early0, late0), (early1, late1), (early2, late2))):
                rows = [u + d for u, d in zip(rows_at(early, b, z), rows_at(late, b, z))]
                put_plane(fine, (b * CF + i, z), rows)
            put_plane(fine, (b * CF + CF - 1, z), rows_at(relaxed, b, z))


def coarse_kernel(
    below, above, arrived, lo, hi, change_lo, change_hi, change, relaxed, last, coef, state, source,
    near, far, right, state_out, source_out, leaving,
):
    for z in range(3 * SLAB):
        put_rows(near, (0, z), rows_at(below, z))
        if z >= SLAB:
            put_rows(near, (0, INNER + z), rows_at(above, z))
    for z in range(3 * SLAB):
        part, at = divmod(z, SLAB)
        if part == 1:
            rows = rows_at(arrived, at)
        else:
            halo, moved = (lo, change_lo) if part == 0 else (hi, change_hi)
            rows = [u + d for u, d in zip(rows_at(halo, UP_START + at), rows_at(moved, 0, at))]
        put_rows(near, (1, SLAB + z), [u + d for u, d in zip(rows, rows_at(near, 0, SLAB + z))])
    shift = HALO - INNER - 1
    wide_step(coef, COARSE, (0,), near, far, right, 0, SLAB + 2 * INNER, shift)
    for z in range(SLAB):
        point = [u + d for u, d in zip(rows_at(relaxed, 0, z), rows_at(change, 0, z))]
        put_plane(state_out, (0, z), [u + d for u, d in zip(point, rows_at(near, 0, INNER + z))])
        put_plane(state_out, (1, z), rows_at(last, z))
    state_copy = pltpu.make_async_copy(state_out, state, leaving.at[0])
    state_copy.start()
    wide_step(coef, COARSE, (0,), near, far, right, SLAB, SLAB + 3 * SLAB, shift)
    wide_step(coef, COARSEST, (1,), near, far, right, SLAB, SLAB + 3 * SLAB, shift)
    for z in range(SLAB):
        both = zip(rows_at(near, 0, INNER + z), rows_at(last, z), rows_at(near, 1, INNER + z))
        put_plane(source_out, (0, z), [(d + u) - w for d, u, w in both])
    source_copy = pltpu.make_async_copy(source_out, source, leaving.at[1])
    source_copy.start()
    state_copy.wait()
    source_copy.wait()


def on_device(forcing, c_guess, initial, porosity, permeability):
    four = (SLAB,) + PLANE
    both = (2,) + four
    last_time = lax.axis_index("tm") == lax.axis_size("tm") - 1

    arrived = shifted(jnp.where(last_time, initial, c_guess[1]), 1, 0)
    later = (2, CF - 1, EDGE) + PLANE
    message = (MESSAGE,) + PLANE
    up, down, up_later, down_later, force, guess, field, half = call(
        prepare_kernel, "prepare", [message, message, later, later, (2, CF) + four, four, (4,) + four, both],
        forcing, c_guess, porosity, permeability, anywhere=4,
        scratch=[forcing.shape, initial.shape, porosity.shape, permeability.shape, pltpu.SemaphoreType.DMA((4,))],
    )
    up, down, start = call(complete_kernel, "complete", [message, message, both], arrived, guess, up, down)
    lo, hi = shifted(up, 0, 1), shifted(down, 0, -1)
    force_lo, force_hi = shifted(up_later, 0, 1), shifted(down_later, 0, -1)
    coef, state = call(
        first_kernel, "first", [(8, REACH) + PLANE, both], start, lo, hi, force, field, scratch=scratch_of(2)
    )
    half_lo, half_hi = shifted(half, 0, 2), shifted(half, 0, -2)
    packed = (2, PACK) + PLANE
    early = [state]
    for section in range(1, CF):
        state_lo, state_hi = shifted(state, 0, 1), shifted(state, 0, -1)
        (state,) = call(
            early_kernel(section), f"early{section}", [both], state, state_lo, state_hi, force, force_lo, force_hi,
            coef, scratch=scratch_of(2),
        )
        early.append(state)
        if section == 1:
            half_up, half_down = call(
                pack_field_kernel, "pack_field", [packed, packed], half, lo, hi, half_lo, half_hi, state
            )
            half_far_lo, half_far_hi = shifted(half_up, 0, 4), shifted(half_down, 0, -4)
    relaxed = early[-1]

    (on,) = call(pass_kernel, "pass", [four], relaxed, initial)
    arrived = shifted(on, 1, 0)
    (share,) = call(
        share_kernel, "share", [(2, 2 * (PACK + SLAB)) + PLANE], half_lo, half_hi, half_far_lo, half_far_hi, relaxed
    )
    other_share = swapped(share)
    (change,) = call(change_kernel, "change", [both], arrived, relaxed, start)
    change_lo, change_hi = shifted(change, 0, 1), shifted(change, 0, -1)
    two_lo, two_hi = shifted(change, 0, 2), shifted(change, 0, -2)
    change_up, change_down = call(pack_kernel, "pack", [packed, packed], change, change_lo, change_hi, two_lo, two_hi)
    far_lo, far_hi = shifted(change_up, 0, 4), shifted(change_down, 0, -4)
    (coef,) = call(
        wide_kernel, "wide", [(10, SPAN - 2) + PLANE], field, lo, hi, share, other_share,
        scratch=[(4, SPAN) + PLANE],
    )
    late0, late1, late2, changed, last, on = call(
        late_kernel, "late", [both] * 4 + [four, (3 * SLAB,) + PLANE], change, change_lo, change_hi, two_lo, two_hi,
        far_lo, far_hi, relaxed, coef, scratch=[(2, SPAN) + PLANE] * 3,
    )
    below, above = shifted(on, 1, 1), shifted(on, 1, -1)
    (fine_state,) = call(fine_kernel, "fine", [forcing.shape], *early, late0, late1, late2)
    coarse_state, coarse_source = call(
        coarse_kernel, "coarse", [(2,) + initial.shape, (1,) + initial.shape], below, above, arrived, lo, hi,
        change_lo, change_hi, changed, relaxed, last, coef, stored=True,
        scratch=[(2, SLAB + 2 * INNER) + PLANE] * 3
        + [(2,) + initial.shape, (1,) + initial.shape, pltpu.SemaphoreType.DMA((2,))],
    )
    return (fine_state, coarse_state, coarse_source)


def solution(mesh):
    return jax.shard_map(
        on_device,
        mesh=mesh,
        in_specs=(
            P("tm", "space", None, None),
            P("tm", "space", None, None),
            P("space", None, None),
            P("space", None, None),
            P(None, "space", None, None),
        ),
        out_specs=(
            P("tm", "space", None, None),
            P("tm", "space", None, None),
            P("tm", "space", None, None),
        ),
        check_vma=False,
    )
```

```python
import jax
import jax.numpy as jnp
from jax import lax
from jax.experimental import pallas as pl
from jax.experimental.pallas import tpu as pltpu
from jax.sharding import PartitionSpec as P

CF = 4
SLAB = 4
EDGE = SLAB - 1
ROWS = 4

storage_rate = 2.0


def shifted(value, dt, ds):
    times = lax.axis_size("tm")
    slabs = lax.axis_size("space")
    pairs = [
        (t * slabs + s, ((t + dt) % times) * slabs + (s + ds) % slabs)
        for t in range(times)
        for s in range(slabs)
    ]
    return lax.ppermute(value, ("tm", "space"), pairs)


def swapped(value):
    return lax.ppermute(value, "tm", [(t, t ^ 1) for t in range(lax.axis_size("tm"))])


def call(kernel, name, outs, *args, scratch=(), anywhere=0, stored=False):
    held = [
        pltpu.with_memory_space_constraint(a, pltpu.HBM if i < anywhere else pltpu.VMEM) for i, a in enumerate(args)
    ]
    inside = pl.BlockSpec(memory_space=pltpu.VMEM)
    outside = pl.BlockSpec(memory_space=pl.ANY)
    return pl.pallas_call(
        kernel,
        out_shape=[(pltpu.HBM if stored else pltpu.VMEM)(shape, jnp.float32) for shape in outs],
        in_specs=[outside if i < anywhere else inside for i in range(len(args))],
        out_specs=[outside if stored else inside] * len(outs),
        scratch_shapes=[pltpu.VMEM(s, jnp.float32) if isinstance(s, tuple) else s for s in scratch],
        name=name,
        compiler_params=pltpu.CompilerParams(vmem_limit_bytes=16 * 2**20),
    )(*held)


PLANE = (ROWS, 8, 128)


def plane_of(ref, *at):
    return [ref[(*at, pl.ds(j, 8, stride=ROWS), slice(None))] for j in range(ROWS)]


def put_plane(ref, at, rows):
    for j in range(ROWS):
        ref[(*at, pl.ds(j, 8, stride=ROWS), slice(None))] = rows[j]


def x_lower(v):
    return pltpu.roll(v, 1, 1)


def x_upper(v):
    return pltpu.roll(v, 127, 1)


def y_lower(rows):
    return [pltpu.roll(rows[-1], 1, 0)] + rows[:-1]


def y_upper(rows):
    return rows[1:] + [pltpu.roll(rows[0], 7, 0)]


def rows_at(ref, *at):
    return [ref[(*at, j)] for j in range(ROWS)]


def put_rows(ref, at, rows):
    for j in range(ROWS):
        ref[(*at, j)] = rows[j]


WEST, EAST, SOUTH, NORTH, BELOW, ABOVE, STORAGE, FINE, COARSE, COARSEST = range(10)
REACH = SLAB + 2 * EDGE
FACTORS = {FINE: 1.0, COARSE: 1.0 / CF, COARSEST: 1.0 / (2 * CF)}


def step(coef, levels, window, source, put, near, far, right):
    count = len(levels)
    for turn in range(4):
        planes = REACH - 2 * turn
        out = [near, far, near, None][turn]
        held = [None, near, far, near][turn]
        for p in range(planes):
            at = p + turn
            links = [rows_at(coef, kind, at) for kind in range(6)]
            inverses = {level: rows_at(coef, level, at) for level in set(levels)}
            for b in range(count):
                if turn == 0:
                    lower, middle, upper = window(b, p), window(b, p + 1), window(b, p + 2)
                    stored = rows_at(coef, STORAGE, at)
                    factor = FACTORS[levels[b]]
                    if factor != 1.0:
                        stored = [s * factor for s in stored]
                    rhs = [s * v for s, v in zip(stored, middle)]
                    if source is not None:
                        rhs = [r + f for r, f in zip(rhs, source(b, p))]
                    if 0 < p < planes - 1:
                        put_rows(right, (b, p - 1), rhs)
                else:
                    lower, middle, upper = [rows_at(held, b, p + k) for k in range(3)]
                    rhs = rows_at(right, b, at - 1)
                south_of, north_of = y_lower(middle), y_upper(middle)
                result = []
                for j in range(ROWS):
                    west, east, south, north, below, above = [link[j] for link in links]
                    total = rhs[j] + (west * x_lower(middle[j]) + east * x_upper(middle[j]))
                    total = total + (south * south_of[j] + north * north_of[j])
                    total = total + (below * lower[j] + above * upper[j])
                    result.append(total * inverses[levels[b]][j])
                if out is None:
                    put(b, p, result)
                else:
                    put_rows(out, (b, p), result)


def scratch_of(count):
    return [(count, 10) + PLANE, (count, 8) + PLANE, (count, 8) + PLANE]


def windows(lo, own, hi):
    def window(b, p):
        if p < SLAB:
            return rows_at(lo, b, p)
        if p < 2 * SLAB:
            return rows_at(own, b, p - SLAB)
        return rows_at(hi, b, p - 2 * SLAB)

    return window


UP_START, UP_FORCE, UP_FIELD = 0, 8, 14
MESSAGE = 30
X, Y, Z, PORE = range(4)


def own_half(first, second):
    even = lax.rem(lax.axis_index("tm"), 2) == 0
    return [jnp.where(even, a, b) for a, b in zip(first, second)]


def prepare_kernel(
    forcing, guess, porosity, permeability, up, down, up_later, down_later, force, start, field, half,
    force_in, guess_in, pore_in, perm_in, arrivals,
):
    copies = [
        pltpu.make_async_copy(source, target, arrivals.at[i])
        for i, (source, target) in enumerate(
            ((guess.at[0], guess_in), (porosity, pore_in), (permeability, perm_in), (forcing, force_in))
        )
    ]
    for copy in copies:
        copy.start()
    for copy in copies[:3]:
        copy.wait()
    for z in range(SLAB):
        rows = plane_of(guess_in, z)
        put_rows(start, (z,), rows)
        for target in (up, down):
            put_rows(target, (UP_START + SLAB + z,), rows)
        for kind in range(4):
            rows = plane_of(pore_in, z) if kind == PORE else plane_of(perm_in, kind, z)
            put_rows(field, (kind, z), rows)
            for target in (up, down):
                put_rows(target, (UP_FIELD + SLAB * kind + z,), rows)
        for kind in range(2):
            put_rows(half, (kind, z), own_half(rows_at(field, kind, z), rows_at(field, kind + 2, z)))
    copies[3].wait()
    for z in range(SLAB):
        for b in range(2):
            for i in range(CF):
                rows = plane_of(force_in, b * CF + i, z)
                put_rows(force, (b, i, z), rows)
                for target, later, skip in ((up, up_later, 1), (down, down_later, 0)):
                    if 0 <= z - skip < EDGE:
                        if i == 0:
                            put_rows(target, (UP_FORCE + EDGE * b + z - skip,), rows)
                        else:
                            put_rows(later, (b, i - 1, z - skip), rows)


def complete_kernel(arrived, guess, up_part, down_part, up, down, start):
    for z in range(SLAB):
        rows = plane_of(arrived, z)
        put_rows(start, (0, z), rows)
        put_rows(start, (1, z), rows_at(guess, z))
        put_rows(up, (UP_START + z,), rows)
        put_rows(down, (UP_START + z,), rows)
    up[SLAB:] = up_part[SLAB:]
    down[SLAB:] = down_part[SLAB:]


def harmonic(lower, upper):
    return [2.0 * a * b / (a + b) for a, b in zip(lower, upper)]


def face_terms(held):
    column = lax.broadcasted_iota(jnp.int32, (8, 128), 1)
    row = lax.broadcasted_iota(jnp.int32, (8, 128), 0)
    zero = jnp.zeros((8, 128), jnp.float32)
    kx, ky, kz = [held(kind, 0) for kind in (X, Y, Z)]
    side = harmonic(kx, [x_upper(k) for k in kx])
    east_link = [jnp.where(column == 127, zero, v) for v in side]
    east = [jnp.where(column == 127, k, v) for k, v in zip(kx, side)]
    side = [x_lower(v) for v in side]
    west_link = [jnp.where(column == 0, zero, v) for v in side]
    west = [jnp.where(column == 0, k, v) for k, v in zip(kx, side)]
    side = harmonic(ky, y_upper(ky))
    north_link, north = list(side), list(side)
    north_link[-1] = jnp.where(row == 7, zero, side[-1])
    north[-1] = jnp.where(row == 7, ky[-1], side[-1])
    side = y_lower(side)
    south_link, south = list(side), list(side)
    south_link[0] = jnp.where(row == 0, zero, side[0])
    south[0] = jnp.where(row == 0, ky[0], side[0])
    links = [west_link, east_link, south_link, north_link]
    return links, [west, east, south, north], kz


def put_coefficients(coef, p, height, held, levels):
    last = SLAB * lax.axis_size("space") - 1
    zero = jnp.zeros((8, 128), jnp.float32)
    links, sides, kz = face_terms(held)
    below = harmonic(held(Z, -1), kz)
    above = harmonic(kz, held(Z, 1))
    floor, top = height == 0, height == last
    links.append([jnp.where(floor, zero, v) for v in below])
    links.append([jnp.where(top, zero, v) for v in above])
    below = [jnp.where(floor, k, v) for k, v in zip(kz, below)]
    above = [jnp.where(top, k, v) for k, v in zip(kz, above)]
    west, east, south, north = sides
    for kind, rows in enumerate(links):
        put_rows(coef, (kind, p), rows)
    stored = [storage_rate * v for v in held(PORE, 0)]
    put_rows(coef, (STORAGE, p), stored)
    for j in range(ROWS):
        coupling = ((west[j] + east[j]) + (south[j] + north[j])) + (below[j] + above[j])
        for level in levels:
            coef[level, p, j] = 1.0 / (stored[j] * FACTORS[level] + coupling)


def first_kernel(start, lo, hi, force, field, coef, state, up, down, near, far, right):
    position = lax.axis_index("space")
    cells = SLAB * lax.axis_size("space")
    for p in range(REACH):

        def held(kind, k, p=p):
            part, at = divmod(p + 1 + k, SLAB)
            if part == 1:
                return rows_at(field, kind, at)
            return rows_at([lo, None, hi][part], UP_FIELD + SLAB * kind + at)

        height = lax.rem(position * SLAB + p - EDGE + cells, cells)
        put_coefficients(coef, p, height, held, (FINE,))

    def window(b, p):
        part, at = divmod(p, SLAB)
        if part == 1:
            return rows_at(start, b, at)
        return rows_at([lo, None, hi][part], UP_START + SLAB * b + at)

    def source(b, p):
        if p < EDGE:
            return rows_at(lo, UP_FORCE + EDGE * b + p)
        if p < EDGE + SLAB:
            return rows_at(force, b, 0, p - EDGE)
        return rows_at(hi, UP_FORCE + EDGE * b + p - EDGE - SLAB)

    def put(b, p, rows):
        for target in (state, up, down):
            put_rows(target, (b, p), rows)

    step(coef, [FINE, FINE], window, source, put, near, far, right)
    for part, target in ((lo, up), (hi, down)):
        for k in range(2):
            for z in range(SLAB):
                at = UP_FIELD + SLAB * k + z
                put_rows(target, (2 + k, z), own_half(rows_at(part, at), rows_at(part, at + 2 * SLAB)))


def early_kernel(section):
    def kernel(own, lo, hi, force, force_lo, force_hi, coef, state, near, far, right):
        def source(b, p):
            if p < EDGE:
                return rows_at(force_lo, b, section - 1, p)
            if p < EDGE + SLAB:
                return rows_at(force, b, section, p - EDGE)
            return rows_at(force_hi, b, section - 1, p - EDGE - SLAB)

        put = lambda b, p, rows: put_rows(state, (b, p), rows)
        step(coef, [FINE, FINE], windows(lo, own, hi), source, put, near, far, right)

    return kernel


def pass_kernel(relaxed, initial, on):
    last_time = lax.axis_index("tm") == lax.axis_size("tm") - 1
    for z in range(SLAB):
        rows = [jnp.where(last_time, a, b) for a, b in zip(plane_of(initial, z), rows_at(relaxed, 1, z))]
        put_rows(on, (z,), rows)


def change_kernel(arrived, relaxed, start, change):
    for z in range(SLAB):
        for j in range(ROWS):
            change[0, z, j] = arrived[z, j] - start[0, z, j]
            change[1, z, j] = relaxed[0, z, j] - start[1, z, j]


HALO = 24
SPAN = 2 * HALO + SLAB
PACK = 16
INNER = 8


THIN = PACK - SLAB


def pack_kernel(own, lo, hi, lo_two, hi_two, up, down):
    for z in range(SLAB):
        parts = [rows_at(part, 0, z) for part in (lo_two, lo, own, hi, hi_two)]
        for i in range(4):
            put_rows(up, (SLAB * i + z,), parts[i])
            put_rows(down, (SLAB * i + z,), parts[i + 1])
        for i, part in enumerate((lo, own, hi)):
            rows = rows_at(part, 1, z)
            put_rows(up, (PACK + SLAB * i + z,), rows)
            put_rows(down, (PACK + SLAB * i + z,), rows)


def pack_field_kernel(own, lo, hi, lo_two, hi_two, after, up, down):
    for k in range(2):
        for z in range(SLAB):
            at = UP_FIELD + SLAB * k + z
            near_lo = own_half(rows_at(lo, at), rows_at(lo, at + 2 * SLAB))
            near_hi = own_half(rows_at(hi, at), rows_at(hi, at + 2 * SLAB))
            parts = [rows_at(lo_two, 2 + k, z), near_lo, rows_at(own, k, z), near_hi, rows_at(hi_two, 2 + k, z)]
            for i in range(4):
                put_rows(up, (k, SLAB * i + z), parts[i])
                put_rows(down, (k, SLAB * i + z), parts[i + 1])


def share_kernel(lo_two, hi_two, lo_far, hi_far, after, share):
    share[:, :PACK] = lo_far[...]
    share[:, PACK : PACK + SLAB] = lo_two[2:]
    share[:, PACK + SLAB : PACK + 2 * SLAB] = hi_two[2:]
    share[:, PACK + 2 * SLAB :] = hi_far[...]


def wide_kernel(own, lo, hi, mine, other, coef, wide):
    for k in range(2):
        for z in range(PACK + SLAB):
            for at, target in ((z, z), (PACK + SLAB + z, HALO + 2 * SLAB + z)):
                a, b = rows_at(mine, k, at), rows_at(other, k, at)
                put_rows(wide, (k, target), own_half(a, b))
                put_rows(wide, (k + 2, target), own_half(b, a))
    for k in range(4):
        for z in range(SLAB):
            at = UP_FIELD + SLAB * k + z
            put_rows(wide, (k, HALO - SLAB + z), rows_at(lo, at))
            put_rows(wide, (k, HALO + z), rows_at(own, k, z))
            put_rows(wide, (k, HALO + SLAB + z), rows_at(hi, at))
    position = lax.axis_index("space")
    cells = SLAB * lax.axis_size("space")

    def body(start, size):
        for k in range(size):
            p = start + k
            height = lax.rem(position * SLAB + p + (cells - HALO + 1), cells)
            held = lambda kind, i, p=p: rows_at(wide, kind, p + 1 + i)
            put_coefficients(coef, p, height, held, (FINE, COARSE, COARSEST))

    in_chunks(SPAN - 2, 10, body)


CHUNK = 26


def in_chunks(count, chunk, body):
    pieces = max(1, round(count / chunk))
    size = -(-count // pieces)
    if pieces == 1:
        body(0, size)
        return

    def turn(i, carry):
        body(jnp.minimum(i * size, count - size), size)
        return carry

    lax.fori_loop(0, pieces, turn, 0)


def sweep_planes(coef, level, blocks, old, new, right, low, high, shift, first):
    factor = FACTORS[level]

    def body(start, size):
        for k in range(size):
            w = low + start + k
            at = w + shift
            links = [rows_at(coef, kind, at) for kind in range(6)]
            inverse = rows_at(coef, level, at)
            if first:
                stored = rows_at(coef, STORAGE, at)
                if factor != 1.0:
                    stored = [s * factor for s in stored]
            for b in blocks:
                lower, middle, upper = [rows_at(old, b, w + i) for i in (-1, 0, 1)]
                if first:
                    rhs = [s * v for s, v in zip(stored, middle)]
                    put_rows(right, (b, w), rhs)
                else:
                    rhs = rows_at(right, b, w)
                south_of, north_of = y_lower(middle), y_upper(middle)
                for j in range(ROWS):
                    west, east, south, north, below, above = [link[j] for link in links]
                    total = rhs[j] + (west * x_lower(middle[j]) + east * x_upper(middle[j]))
                    total = total + (south * south_of[j] + north * north_of[j])
                    total = total + (below * lower[j] + above * upper[j])
                    new[b, w, j] = total * inverse[j]

    in_chunks(high - low, CHUNK * 2 // len(blocks), body)


def wide_step(coef, level, blocks, near, far, right, low, high, shift):
    for turn in range(4):
        old, new = (near, far) if turn % 2 == 0 else (far, near)
        sweep_planes(coef, level, blocks, old, new, right, low + turn + 1, high - turn - 1, shift, turn == 0)


def late_kernel(
    own, lo, hi, lo_two, hi_two, lo_far, hi_far, relaxed, coef, late0, late1, late2, change, last, on, near, far, right
):
    last_time = lax.axis_index("tm") == lax.axis_size("tm") - 1
    for z in range(PACK):
        put_rows(near, (0, z), rows_at(lo_far, z))
        put_rows(near, (0, HALO + 3 * SLAB + z), rows_at(hi_far, z))
    empty = [jnp.zeros((8, 128), jnp.float32)] * ROWS
    for z in range(SLAB):
        put_rows(near, (1, z), empty)
        put_rows(near, (1, SPAN - SLAB + z), empty)
    for z in range(THIN):
        put_rows(near, (1, SLAB + z), rows_at(lo_far, PACK + z))
        put_rows(near, (1, HALO + 3 * SLAB + z), rows_at(hi_far, PACK + z))
    for b in range(2):
        for i, part in enumerate((lo_two, lo, own, hi, hi_two)):
            for z in range(SLAB):
                put_rows(near, (b, HALO + SLAB * (i - 2) + z), rows_at(part, b, z))
    for section, late in enumerate((late0, late1, late2, change)):
        wide_step(coef, FINE, (0, 1), near, far, right, SLAB * section, SPAN - SLAB * section, -1)
        for b in range(2):
            for z in range(SLAB):
                put_rows(late, (b, z), rows_at(near, b, HALO + z))
    wide_step(coef, COARSE, (0,), near, far, right, HALO - INNER, HALO + SLAB + INNER, -1)
    for z in range(3 * SLAB):
        w = HALO - SLAB + z
        rows = [a + d for a, d in zip(rows_at(near, 1, w), rows_at(near, 0, w))]
        put_rows(on, (z,), [jnp.where(last_time, 0.0, d) for d in rows])
        if SLAB <= z < 2 * SLAB:
            put_rows(last, (z - SLAB,), [u + d for u, d in zip(rows_at(relaxed, 1, z - SLAB), rows)])


def fine_kernel(early0, early1, early2, relaxed, late0, late1, late2, fine):
    for b in range(2):
        for z in range(SLAB):
            for i, (early, late) in enumerate(((early0, late0), (early1, late1), (early2, late2))):
                rows = [u + d for u, d in zip(rows_at(early, b, z), rows_at(late, b, z))]
                put_plane(fine, (b * CF + i, z), rows)
            put_plane(fine, (b * CF + CF - 1, z), rows_at(relaxed, b, z))


def coarse_kernel(
    below, above, arrived, lo, hi, change_lo, change_hi, change, relaxed, last, coef, state, source,
    near, far, right, state_out, source_out, leaving,
):
    for z in range(3 * SLAB):
        put_rows(near, (0, z), rows_at(below, z))
        if z >= SLAB:
            put_rows(near, (0, INNER + z), rows_at(above, z))
    for z in range(3 * SLAB):
        part, at = divmod(z, SLAB)
        if part == 1:
            rows = rows_at(arrived, at)
        else:
            halo, moved = (lo, change_lo) if part == 0 else (hi, change_hi)
            rows = [u + d for u, d in zip(rows_at(halo, UP_START + at), rows_at(moved, 0, at))]
        put_rows(near, (1, SLAB + z), [u + d for u, d in zip(rows, rows_at(near, 0, SLAB + z))])
    shift = HALO - INNER - 1
    wide_step(coef, COARSE, (0,), near, far, right, 0, SLAB + 2 * INNER, shift)
    for z in range(SLAB):
        point = [u + d for u, d in zip(rows_at(relaxed, 0, z), rows_at(change, 0, z))]
        put_plane(state_out, (0, z), [u + d for u, d in zip(point, rows_at(near, 0, INNER + z))])
        put_plane(state_out, (1, z), rows_at(last, z))
    state_copy = pltpu.make_async_copy(state_out, state, leaving.at[0])
    state_copy.start()
    wide_step(coef, COARSE, (0,), near, far, right, SLAB, SLAB + 3 * SLAB, shift)
    wide_step(coef, COARSEST, (1,), near, far, right, SLAB, SLAB + 3 * SLAB, shift)
    for z in range(SLAB):
        both = zip(rows_at(near, 0, INNER + z), rows_at(last, z), rows_at(near, 1, INNER + z))
        put_plane(source_out, (0, z), [(d + u) - w for d, u, w in both])
    source_copy = pltpu.make_async_copy(source_out, source, leaving.at[1])
    source_copy.start()
    state_copy.wait()
    source_copy.wait()


def on_device(forcing, c_guess, initial, porosity, permeability):
    four = (SLAB,) + PLANE
    both = (2,) + four
    last_time = lax.axis_index("tm") == lax.axis_size("tm") - 1

    arrived = shifted(jnp.where(last_time, initial, c_guess[1]), 1, 0)
    later = (2, CF - 1, EDGE) + PLANE
    message = (MESSAGE,) + PLANE
    up, down, up_later, down_later, force, guess, field, half = call(
        prepare_kernel, "prepare", [message, message, later, later, (2, CF) + four, four, (4,) + four, both],
        forcing, c_guess, porosity, permeability, anywhere=4,
        scratch=[forcing.shape, initial.shape, porosity.shape, permeability.shape, pltpu.SemaphoreType.DMA((4,))],
    )
    up, down, start = call(complete_kernel, "complete", [message, message, both], arrived, guess, up, down)
    lo, hi = shifted(up, 0, 1), shifted(down, 0, -1)
    force_lo, force_hi = shifted(up_later, 0, 1), shifted(down_later, 0, -1)
    coef, state, up, down = call(
        first_kernel, "first", [(8, REACH) + PLANE, both, (4,) + four, (4,) + four], start, lo, hi, force, field, scratch=scratch_of(2)
    )
    packed = (2, PACK) + PLANE
    early = [state]
    for section in range(1, CF):
        if section == 1:
            state_lo, state_hi = half_lo, half_hi = shifted(up, 0, 1), shifted(down, 0, -1)
        else:
            state_lo, state_hi = shifted(state, 0, 1), shifted(state, 0, -1)
        (state,) = call(
            early_kernel(section), f"early{section}", [both], state, state_lo, state_hi, force, force_lo, force_hi,
            coef, scratch=scratch_of(2),
        )
        early.append(state)
        if section == 1:
            half_up, half_down = call(
                pack_field_kernel, "pack_field", [packed, packed], half, lo, hi, half_lo, half_hi, state
            )
            half_far_lo, half_far_hi = shifted(half_up, 0, 4), shifted(half_down, 0, -4)
    relaxed = early[-1]

    (on,) = call(pass_kernel, "pass", [four], relaxed, initial)
    arrived = shifted(on, 1, 0)
    (share,) = call(
        share_kernel, "share", [(2, 2 * (PACK + SLAB)) + PLANE], half_lo, half_hi, half_far_lo, half_far_hi, relaxed
    )
    other_share = swapped(share)
    (change,) = call(change_kernel, "change", [both], arrived, relaxed, start)
    change_lo, change_hi = shifted(change, 0, 1), shifted(change, 0, -1)
    two_lo, two_hi = shifted(change, 0, 2), shifted(change, 0, -2)
    packed = (PACK + THIN,) + PLANE
    change_up, change_down = call(pack_kernel, "pack", [packed, packed], change, change_lo, change_hi, two_lo, two_hi)
    far_lo, far_hi = shifted(change_up, 0, 4), shifted(change_down, 0, -4)
    (coef,) = call(
        wide_kernel, "wide", [(10, SPAN - 2) + PLANE], field, lo, hi, share, other_share,
        scratch=[(4, SPAN) + PLANE],
    )
    late0, late1, late2, changed, last, on = call(
        late_kernel, "late", [both] * 4 + [four, (3 * SLAB,) + PLANE], change, change_lo, change_hi, two_lo, two_hi,
        far_lo, far_hi, relaxed, coef, scratch=[(2, SPAN) + PLANE] * 3,
    )
    below, above = shifted(on, 1, 1), shifted(on, 1, -1)
    (fine_state,) = call(fine_kernel, "fine", [forcing.shape], *early, late0, late1, late2)
    coarse_state, coarse_source = call(
        coarse_kernel, "coarse", [(2,) + initial.shape, (1,) + initial.shape], below, above, arrived, lo, hi,
        change_lo, change_hi, changed, relaxed, last, coef, stored=True,
        scratch=[(2, SLAB + 2 * INNER) + PLANE] * 3
        + [(2,) + initial.shape, (1,) + initial.shape, pltpu.SemaphoreType.DMA((2,))],
    )
    return (fine_state, coarse_state, coarse_source)


def solution(mesh):
    return jax.shard_map(
        on_device,
        mesh=mesh,
        in_specs=(
            P("tm", "space", None, None),
            P("tm", "space", None, None),
            P("space", None, None),
            P("space", None, None),
            P(None, "space", None, None),
        ),
        out_specs=(
            P("tm", "space", None, None),
            P("tm", "space", None, None),
            P("tm", "space", None, None),
        ),
        check_vma=False,
    )
```
